32 devices in a mesh: groups: 2 (over y), dom: 4 (over x, core), sub: 4 (over z).
Axes of the slice: x: 2, y: 2, z: 4, core: 2. Of those that a mesh axis runs over, the one named last changes fastest.
Arguments:
- node_states: float32 [8192, 512], P(('groups', 'dom', 'sub')), parts along dimension 0, may hold values from -6 to 6
- node_pre: float32 [8192, 512], P(('groups', 'dom', 'sub')), parts along dimension 0, may hold values from -6 to 6
- edge_states: float32 [4096, 512], P(('groups', 'dom', 'sub')), parts along dimension 0, may hold values from -6 to 6
- edge_pre: float32 [4096, 512], P(('groups', 'dom', 'sub')), parts along dimension 0, may hold values from -6 to 6
- node_cotangent: float32 [8192, 512], P(('groups', 'dom', 'sub')), parts along dimension 0, may hold values from -6 to 6
- edge_cotangent: float32 [4096, 512], P(('groups', 'dom', 'sub')), parts along dimension 0, may hold values from -6 to 6
- endpoints: int32 [2, 4096], P(None, ('groups', 'dom', 'sub')), parts along dimension 1, may hold values from 0 to 319, as said below
- send_lists: int32 [32, 4, 16], P(('groups', 'dom', 'sub')), parts along dimension 0, may hold values from 0 to 255, as said below
- node_counts: int32 [32], P(('groups', 'dom', 'sub')), parts along dimension 0, may hold values from 128 to 256
- edge_blocks: int32 [32], P(('groups', 'dom', 'sub')), parts along dimension 0, may hold values from 1 to 1
- edge_first: float32 [1536, 512], P(('dom', 'sub')), may hold values from -0.15625 to 0.15625
- edge_second: float32 [512, 512], P(('dom', 'sub')), may hold values from -0.25 to 0.25
- edge_bias: float32 [512], P(('dom', 'sub')), may hold values from -3 to 3
- edge_gain: float32 [512], P(('dom', 'sub')), may hold values from 0.5 to 1.5
- edge_shift: float32 [512], P(('dom', 'sub')), may hold values from -3 to 3
- node_first: float32 [1024, 512], P(('dom', 'sub')), may hold values from -0.1875 to 0.1875
- node_second: float32 [512, 512], P(('dom', 'sub')), may hold values from -0.25 to 0.25
- node_bias: float32 [512], P(('dom', 'sub')), may hold values from -3 to 3
- node_gain: float32 [512], P(('dom', 'sub')), may hold values from 0.5 to 1.5
Outputs:
- edge_grads: float32 [4096, 512], P(('groups', 'dom', 'sub')), parts along dimension 0
- node_grads: float32 [8192, 512], P(('groups', 'dom', 'sub')), parts along dimension 0
- edge_first_grad: float32 [3072, 512], P(('groups', 'dom', 'sub')), parts along dimension 0
- edge_second_grad: float32 [1024, 512], P(('groups', 'dom', 'sub')), parts along dimension 0
- node_first_grad: float32 [2048, 512], P(('groups', 'dom', 'sub')), parts along dimension 0
- node_second_grad: float32 [1024, 512], P(('groups', 'dom', 'sub')), parts along dimension 0
The draws below stay inside these ranges and needn't reach their ends.
There are 2 independent parts, one for each index of `groups`. The reference program is written for one: setup_inputs(seed, part) draws one part's arguments, and reference() takes and returns one part's arrays. A program takes and returns all parts, laid end to end along the dimension named above; an argument that names none is the same for every part. Nothing has to cross between parts.
Inputs may be any that keep to these rules, and one draw needn't show every extreme that they name: `endpoints`: sender slots are a live local node below node_counts of the device, or a ghost slot 256 + k * 16 + j whose neighbour k exists; receiver slots are live local nodes. `send_lists`: every entry is a live node of its device.
All inputs are finite; a program needn't handle non-finite values.
Results may differ from the reference program's by a relative error of at most 0.0003.
Values sent between devices are 32-bit elements; how exact they have to be, the bound alone decides.
A program may use at most 128 MiB of HBM per device.

```python
import jax
import jax.numpy as jnp
from jax import lax

D = 512
E_DEV = 128
N_DEV = 256
G = 16
DOMS = 4
SUBS = 4
DEVS = 16
BLOCKS = 1
EDGES = 2048
NODES = 4096


def fullest_device(key):
    base = jax.random.fold_in(key, 101)
    first, second = jax.random.split(base)
    return (first, jax.random.randint(second, (), 0, DEVS))


def live_counts(key):
    first, fullest = fullest_device(key)
    counts = jax.random.randint(first, (DEVS,), N_DEV // 2, N_DEV + 1)
    return jnp.where(jnp.arange(DEVS) == fullest, N_DEV, counts).astype(jnp.int32)


def draw_node_counts(key, part):
    return live_counts(key)


def draw_edge_blocks(key, part):
    base = jax.random.fold_in(key, 202)
    first, second = jax.random.split(base)
    blocks = jax.random.randint(first, (DEVS,), max(1, BLOCKS // 2), BLOCKS + 1)
    fullest = jax.random.randint(second, (), 0, DEVS)
    return jnp.where(jnp.arange(DEVS) == fullest, BLOCKS, blocks).astype(jnp.int32)


def draw_send_lists(key, part):
    counts = live_counts(key)
    first, fullest = fullest_device(key)
    stream = jax.random.fold_in(key, 303)
    lists = jax.random.randint(stream, (DEVS, 4, G), 0, counts[:, None, None]).astype(jnp.int32)
    lists = lists.at[fullest, 0, 0].set(N_DEV - 1)
    lists = lists.at[fullest, 0, 1].set(0)
    return lists.astype(jnp.int32)


def draw_endpoints(key, part):
    counts = live_counts(key)
    streams = jax.random.split(jax.random.fold_in(key, 404), 5)
    target = jax.random.randint(streams[0], (DEVS, E_DEV), 0, counts[:, None])
    local_source = jax.random.randint(streams[1], (DEVS, E_DEV), 0, counts[:, None])
    direction = jax.random.randint(streams[2], (DEVS, E_DEV), 0, 4)
    ghost_slot = jax.random.randint(streams[3], (DEVS, E_DEV), 0, G)
    ghost_coin = jax.random.randint(streams[4], (DEVS, E_DEV), 0, 4)
    device = jnp.arange(DEVS)[:, None]
    dom_place = device // SUBS
    sub_place = device % SUBS
    exists = jnp.where(direction == 0, dom_place > 0, jnp.where(direction == 1, dom_place < DOMS - 1, jnp.where(direction == 2, sub_place > 0, sub_place < SUBS - 1)))
    source = jnp.where((ghost_coin == 0) & exists, N_DEV + direction * G + ghost_slot, local_source)
    source = source.at[0, 0].set(N_DEV + 4 * G - 1)
    target = target.at[0, 0].set(0)
    return jnp.stack([source.reshape(-1), target.reshape(-1)]).astype(jnp.int32)


def shard_levels(key, shape, cuts, smallest, largest):
    loudness, own = 1.0, jax.random.fold_in(key, 6)
    for dim, shards_of in cuts:
        draws = jnp.exp(jax.random.uniform(jax.random.fold_in(own, dim), (shards_of,), jnp.float32, smallest / len(cuts), largest / len(cuts)))
        loudness = loudness * jnp.repeat(draws, shape[dim] // shards_of).reshape([-1 if axis == dim else 1 for axis in range(len(shape))])
    return loudness


def bell_draw(stream_key, extent, scale, most, cuts=(), held_as=jnp.bfloat16):
    drawn = jax.random.normal(stream_key, extent, jnp.float32) * scale
    if len(cuts) > 0:
        drawn = shard_levels(stream_key, extent, cuts, -0.22, 0.18) * drawn
    return jnp.clip(drawn, min=-most, max=most).astype(held_as)


def setup_inputs(seed: int = 0, part: int = 0) -> dict:
    seeds = jax.random.split(jax.random.key(seed), 20)
    part_keys = jax.random.split(jax.random.fold_in(seeds[19], part), 20)
    return {
        "node_states": bell_draw(part_keys[0], (NODES, D), 1.0, 6.0, ((0, 16),), jnp.float32),
        "node_pre": bell_draw(part_keys[1], (NODES, D), 1.0, 6.0, ((0, 16),), jnp.float32),
        "edge_states": bell_draw(part_keys[2], (EDGES, D), 1.0, 6.0, ((0, 16),), jnp.float32),
        "edge_pre": bell_draw(part_keys[3], (EDGES, D), 1.0, 6.0, ((0, 16),), jnp.float32),
        "node_cotangent": bell_draw(part_keys[4], (NODES, D), 1.0, 6.0, ((0, 16),), jnp.float32),
        "edge_cotangent": bell_draw(part_keys[5], (EDGES, D), 1.0, 6.0, ((0, 16),), jnp.float32),
        "endpoints": draw_endpoints(jax.random.fold_in(jax.random.fold_in(seeds[19], part), 71), part),
        "send_lists": draw_send_lists(jax.random.fold_in(jax.random.fold_in(seeds[19], part), 71), part),
        "node_counts": draw_node_counts(jax.random.fold_in(jax.random.fold_in(seeds[19], part), 71), part),
        "edge_blocks": draw_edge_blocks(jax.random.fold_in(jax.random.fold_in(seeds[19], part), 71), part),
        "edge_first": bell_draw(seeds[10], (3 * D, D), (3 * D) ** -0.5, 0.15625, ((0, 16),), jnp.float32),
        "edge_second": bell_draw(seeds[11], (D, D), D ** -0.5, 0.25, ((0, 16),), jnp.float32),
        "edge_bias": bell_draw(seeds[12], (D,), 0.5, 3.0, ((0, 16),), jnp.float32),
        "edge_gain": jnp.clip(0.5 + 1.0 * jax.random.uniform(seeds[13], (D,), jnp.float32) ** shard_levels(seeds[13], (D,), ((0, 16),), -0.2, 0.2), 0.5, 1.5),
        "edge_shift": bell_draw(seeds[14], (D,), 0.5, 3.0, ((0, 16),), jnp.float32),
        "node_first": bell_draw(seeds[15], (2 * D, D), (2 * D) ** -0.5, 0.1875, ((0, 16),), jnp.float32),
        "node_second": bell_draw(seeds[16], (D, D), D ** -0.5, 0.25, ((0, 16),), jnp.float32),
        "node_bias": bell_draw(seeds[17], (D,), 0.5, 3.0, ((0, 16),), jnp.float32),
        "node_gain": jnp.clip(0.5 + 1.0 * jax.random.uniform(seeds[18], (D,), jnp.float32) ** shard_levels(seeds[18], (D,), ((0, 16),), -0.2, 0.2), 0.5, 1.5),
    }


EPSILON = 1e-05

def matmul(left, right):
    return jnp.dot(left, right, precision=lax.Precision.HIGHEST, preferred_element_type=jnp.float32)

def layer_norm(values):
    center = values - lax.optimization_barrier(jnp.mean(values, axis=-1, keepdims=True))
    inverse = 1.0 / jnp.sqrt(lax.optimization_barrier(jnp.mean(center * center, axis=-1, keepdims=True)) + EPSILON)
    return (center * inverse, inverse)

def norm_back(upstream, normed, inverse):
    first = lax.optimization_barrier(jnp.mean(upstream, axis=-1, keepdims=True))
    second = lax.optimization_barrier(jnp.mean(upstream * normed, axis=-1, keepdims=True))
    return inverse * (upstream - first - normed * second)

def ghost_rows(node_blocks, send_lists):
    sent = jax.vmap(lambda table, picks: jnp.take(table, picks, axis=0))(node_blocks, send_lists)
    sent = sent.reshape(DOMS, SUBS, 4, G, D)
    empty_dom = jnp.zeros((1, SUBS, G, D), jnp.float32)
    empty_sub = jnp.zeros((DOMS, 1, G, D), jnp.float32)
    group_zero = jnp.concatenate([empty_dom, sent[:-1, :, 0]], axis=0)
    group_one = jnp.concatenate([sent[1:, :, 1], empty_dom], axis=0)
    group_two = jnp.concatenate([empty_sub, sent[:, :-1, 2]], axis=1)
    group_three = jnp.concatenate([sent[:, 1:, 3], empty_sub], axis=1)
    stacked = jnp.stack([group_zero, group_one, group_two, group_three], axis=2)
    return stacked.reshape(DEVS, 4 * G, D)

def return_rows(grads):
    shaped = grads.reshape(DOMS, SUBS, 4, G, D)
    empty_dom = jnp.zeros((1, SUBS, G, D), jnp.float32)
    empty_sub = jnp.zeros((DOMS, 1, G, D), jnp.float32)
    list_zero = jnp.concatenate([shaped[1:, :, 0], empty_dom], axis=0)
    list_one = jnp.concatenate([empty_dom, shaped[:-1, :, 1]], axis=0)
    list_two = jnp.concatenate([shaped[:, 1:, 2], empty_sub], axis=1)
    list_three = jnp.concatenate([empty_sub, shaped[:, :-1, 3]], axis=1)
    stacked = jnp.stack([list_zero, list_one, list_two, list_three], axis=2)
    return stacked.reshape(DEVS, 4, G, D)

def reference(node_states, node_pre, edge_states, edge_pre, node_cotangent, edge_cotangent, endpoints, send_lists, node_counts, edge_blocks, edge_first, edge_second, edge_bias, edge_gain, edge_shift, node_first, node_second, node_bias, node_gain):
    node_blocks = node_states.reshape(DEVS, N_DEV, D)
    ghosts = ghost_rows(node_blocks, send_lists)
    device_items = (node_blocks, node_pre.reshape(DEVS, N_DEV, D), edge_states.reshape(DEVS, E_DEV, D), edge_pre.reshape(DEVS, E_DEV, D), node_cotangent.reshape(DEVS, N_DEV, D), edge_cotangent.reshape(DEVS, E_DEV, D), endpoints[0].reshape(DEVS, E_DEV), endpoints[1].reshape(DEVS, E_DEV), node_counts, edge_blocks, ghosts)

    def device_step(totals, device_item):
        states, pre_nodes, edges_here, pre_edges, cot_nodes, cot_edges, source, target, live_count, live_blocks, ghost_here = device_item
        live_nodes = (jnp.arange(N_DEV) < live_count).astype(jnp.float32)[:, None]
        live_edges = (jnp.arange(E_DEV) < live_blocks * 128).astype(jnp.float32)[:, None]
        edge_act = jnp.maximum(pre_edges, 0.0)
        edge_normed, edge_inverse = layer_norm(matmul(edge_act, edge_second) + edge_bias)
        message = (edge_normed * edge_gain + edge_shift) * live_edges
        aggregate = jax.ops.segment_sum(message, target, N_DEV)
        node_act = jnp.maximum(pre_nodes, 0.0)
        node_normed, node_inverse = layer_norm(matmul(node_act, node_second) + node_bias)
        node_upstream = cot_nodes * live_nodes
        node_grad_z = norm_back(node_upstream * node_gain, node_normed, node_inverse)
        node_grad_pre = matmul(node_grad_z, node_second.T) * (pre_nodes > 0).astype(jnp.float32)
        node_input = jnp.concatenate([states, aggregate], axis=1)
        node_grad_input = matmul(node_grad_pre, node_first.T)
        state_grads = node_upstream + node_grad_input[:, :D]
        edge_upstream = (cot_edges + jnp.take(node_grad_input[:, D:], target, axis=0)) * live_edges
        edge_grad_z = norm_back(edge_upstream * edge_gain, edge_normed, edge_inverse)
        edge_grad_pre = matmul(edge_grad_z, edge_second.T) * (pre_edges > 0).astype(jnp.float32)
        extended = jnp.concatenate([states, ghost_here], axis=0)
        features = jnp.concatenate([edges_here, jnp.take(extended, source, axis=0), jnp.take(extended, target, axis=0)], axis=1)
        edge_grad_input = matmul(edge_grad_pre, edge_first.T)
        edge_out = (cot_edges + edge_grad_input[:, :D]) * live_edges
        extended_grads = jax.ops.segment_sum(edge_grad_input[:, D:2 * D], source, N_DEV + 4 * G)
        extended_grads = extended_grads + jax.ops.segment_sum(edge_grad_input[:, 2 * D:], target, N_DEV + 4 * G)
        state_grads = state_grads + extended_grads[:N_DEV]
        returned = extended_grads[N_DEV:].reshape(4, G, D)
        new_totals = (totals[0] + matmul(features.T, edge_grad_pre), totals[1] + matmul(edge_act.T, edge_grad_z), totals[2] + matmul(node_input.T, node_grad_pre), totals[3] + matmul(node_act.T, node_grad_z))
        return (new_totals, (edge_out, state_grads, returned))
    start = (jnp.zeros((3 * D, D), jnp.float32), jnp.zeros((D, D), jnp.float32), jnp.zeros((2 * D, D), jnp.float32), jnp.zeros((D, D), jnp.float32))
    totals, outputs = lax.scan(device_step, start, device_items)
    edge_out, state_grads, returned = outputs
    backward = return_rows(returned)
    added = jax.vmap(lambda rows, picks: jax.ops.segment_sum(rows.reshape(-1, D), picks.reshape(-1), N_DEV))(backward, send_lists)
    state_grads = state_grads + added
    edge_scale = 1.0 / jnp.sqrt(jnp.float32(EDGES))
    node_scale = 1.0 / jnp.sqrt(jnp.float32(NODES))
    return (edge_out.reshape(EDGES, D), state_grads.reshape(NODES, D), totals[0] * edge_scale, totals[1] * edge_scale, totals[2] * node_scale, totals[3] * node_scale)
```

```python
import functools
import math

import jax
import jax.numpy as jnp
from jax import lax
from jax.experimental import pallas as pl
from jax.experimental.pallas import tpu as pltpu
from jax.sharding import PartitionSpec as P

EPSILON = 1e-05


def padded(cells, sides, width):
    for axis, dim in sides:
        count = lax.axis_size(axis)
        ends = count - 1
        head = lax.slice_in_dim(cells, 0, width, axis=dim)
        tail = lax.slice_in_dim(cells, cells.shape[dim] - width, cells.shape[dim], axis=dim)
        cells = jnp.concatenate(
            [
                lax.ppermute(tail, axis, [(i, (i + 1) % count) for i in range(ends)]),
                cells,
                lax.ppermute(head, axis, [((i + 1) % count, i) for i in range(ends)]),
            ],
            axis=dim,
        )
    return cells


def matmul(left, right):
    return jnp.dot(left, right, precision=lax.Precision.HIGHEST, preferred_element_type=jnp.float32)


def inner(left, right):
    return lax.dot_general(
        left,
        right,
        (((0,), (0,)), ((), ())),
        precision=lax.Precision.HIGHEST,
        preferred_element_type=jnp.float32,
    )


def outer_back(left, right):
    return lax.dot_general(
        left,
        right,
        (((1,), (1,)), ((), ())),
        precision=lax.Precision.HIGHEST,
        preferred_element_type=jnp.float32,
    )


def layer_norm(values):
    center = values - jnp.mean(values, axis=-1, keepdims=True)
    inverse = 1.0 / jnp.sqrt(jnp.mean(center * center, axis=-1, keepdims=True) + EPSILON)
    return (center * inverse, inverse)


def norm_back(upstream, normed, inverse):
    first = jnp.mean(upstream, axis=-1, keepdims=True)
    second = jnp.mean(upstream * normed, axis=-1, keepdims=True)
    return inverse * (upstream - first - normed * second)


def plain_shards(
    node_states,
    node_pre,
    edge_states,
    edge_pre,
    node_cotangent,
    edge_cotangent,
    endpoints,
    send_lists,
    node_counts,
    edge_blocks,
    edge_first,
    edge_second,
    edge_bias,
    edge_gain,
    edge_shift,
    node_first,
    node_second,
    node_bias,
    node_gain,
):
    node_rows, width = node_states.shape
    edge_rows = edge_states.shape[0]
    ghost = send_lists.shape[2]
    dom_count = lax.axis_size("dom")
    sub_count = lax.axis_size("sub")
    peer_count = dom_count * sub_count
    lists = send_lists[0]
    outgoing = jnp.take(node_states, lists.reshape(-1), axis=0).reshape(4, ghost, width)
    dom_side = padded(jnp.stack([outgoing[1], outgoing[0]]), (("dom", 0),), 1)
    sub_side = padded(jnp.stack([outgoing[3], outgoing[2]]), (("sub", 0),), 1)
    ghosts = jnp.stack([dom_side[0], dom_side[3], sub_side[0], sub_side[3]])
    ghosts = ghosts.reshape(4 * ghost, width)
    full_node_first, full_node_second, full_node_bias, full_node_gain = (
        lax.all_gather(node_first, ("dom", "sub"), axis=0, tiled=True),
        lax.all_gather(node_second, ("dom", "sub"), axis=0, tiled=True),
        lax.all_gather(node_bias, ("dom", "sub"), axis=0, tiled=True),
        lax.all_gather(node_gain, ("dom", "sub"), axis=0, tiled=True),
    )
    full_edge_first, full_edge_second, full_edge_bias, full_edge_gain, full_edge_shift = (
        lax.all_gather(edge_first, ("dom", "sub"), axis=0, tiled=True),
        lax.all_gather(edge_second, ("dom", "sub"), axis=0, tiled=True),
        lax.all_gather(edge_bias, ("dom", "sub"), axis=0, tiled=True),
        lax.all_gather(edge_gain, ("dom", "sub"), axis=0, tiled=True),
        lax.all_gather(edge_shift, ("dom", "sub"), axis=0, tiled=True),
    )
    live_nodes = (jnp.arange(node_rows) < node_counts[0]).astype(jnp.float32)[:, None]
    live_edges = (jnp.arange(edge_rows) < edge_blocks[0] * 128).astype(jnp.float32)[:, None]
    source = endpoints[0]
    target = endpoints[1]
    edge_scale = 1.0 / math.sqrt(edge_rows * peer_count)
    node_scale = 1.0 / math.sqrt(node_rows * peer_count)
    edge_act = jnp.maximum(edge_pre, 0.0)
    edge_normed, edge_inverse = layer_norm(matmul(edge_act, full_edge_second) + full_edge_bias)
    message = (edge_normed * full_edge_gain + full_edge_shift) * live_edges
    aggregate = jax.ops.segment_sum(message, target, node_rows)
    node_act = jnp.maximum(node_pre, 0.0)
    node_normed, node_inverse = layer_norm(matmul(node_act, full_node_second) + full_node_bias)
    node_upstream = node_cotangent * live_nodes
    node_grad_z = norm_back(node_upstream * full_node_gain, node_normed, node_inverse)
    node_grad_pre = outer_back(node_grad_z, full_node_second) * (node_pre > 0).astype(jnp.float32)
    node_input = jnp.concatenate([node_states, aggregate], axis=1)
    node_first_grad, node_second_grad = (
        lax.psum_scatter(
            inner(node_input, node_grad_pre) * node_scale,
            ("dom", "sub"),
            scatter_dimension=0,
            tiled=True,
        ),
        lax.psum_scatter(
            inner(node_act, node_grad_z) * node_scale,
            ("dom", "sub"),
            scatter_dimension=0,
            tiled=True,
        ),
    )
    node_grad_input = outer_back(node_grad_pre, full_node_first)
    state_grads = node_upstream + node_grad_input[:, :width]
    edge_upstream = (
        edge_cotangent + jnp.take(node_grad_input[:, width:], target, axis=0)
    ) * live_edges
    edge_grad_z = norm_back(edge_upstream * full_edge_gain, edge_normed, edge_inverse)
    edge_grad_pre = outer_back(edge_grad_z, full_edge_second) * (edge_pre > 0).astype(jnp.float32)
    edge_second_grad = lax.psum_scatter(
        inner(edge_act, edge_grad_z) * edge_scale, ("dom", "sub"), scatter_dimension=0, tiled=True
    )
    extended = jnp.concatenate([node_states, ghosts], axis=0)
    features = jnp.concatenate(
        [edge_states, jnp.take(extended, source, axis=0), jnp.take(extended, target, axis=0)],
        axis=1,
    )
    edge_first_grad = lax.psum_scatter(
        inner(features, edge_grad_pre) * edge_scale, ("dom", "sub"), scatter_dimension=0, tiled=True
    )
    edge_grad_input = outer_back(edge_grad_pre, full_edge_first)
    edge_grads = (edge_cotangent + edge_grad_input[:, :width]) * live_edges
    extended_grads = jax.ops.segment_sum(
        edge_grad_input[:, width : 2 * width], source, node_rows + 4 * ghost
    )
    extended_grads = extended_grads + jax.ops.segment_sum(
        edge_grad_input[:, 2 * width :], target, node_rows + 4 * ghost
    )
    state_grads = state_grads + extended_grads[:node_rows]
    ghost_grads = extended_grads[node_rows:].reshape(4, ghost, width)
    dom_back = padded(jnp.stack([ghost_grads[0], ghost_grads[1]]), (("dom", 0),), 1)
    sub_back = padded(jnp.stack([ghost_grads[2], ghost_grads[3]]), (("sub", 0),), 1)
    returned = jnp.stack([dom_back[3], dom_back[0], sub_back[3], sub_back[0]])
    state_grads = state_grads + jax.ops.segment_sum(
        returned.reshape(-1, width), lists.reshape(-1), node_rows
    )
    return (
        edge_grads,
        state_grads,
        edge_first_grad,
        edge_second_grad,
        node_first_grad,
        node_second_grad,
    )


MESH = pl.DeviceIdType.MESH
UNIT = 32


def split(values):
    high = values.astype(jnp.bfloat16)
    return (high, (values - high.astype(jnp.float32)).astype(jnp.bfloat16))


def product(left, right, dims):
    return lax.dot_general(
        left, right, ((dims[:1], dims[1:]), ((), ())), preferred_element_type=jnp.float32
    )


def wide(left, right, dims):
    return (
        product(left[0], right[1], dims)
        + product(left[1], right[0], dims)
        + product(left[0], right[0], dims)
    )


def picked(picks, right, dims=(1, 0)):
    return product(picks, right[1], dims) + product(picks, right[0], dims)


def picks_of(slots, rows, first=0):
    place = lax.broadcasted_iota(jnp.int32, (rows, slots.shape[1]), 0) + first
    ones = jnp.where(place == slots, 1.0, 0.0).astype(jnp.float32)
    return (ones.astype(jnp.bfloat16), ones.T.astype(jnp.bfloat16))


def layer_kernel(
    edge_scale,
    node_scale,
    counts,
    blocks,
    endpoints,
    lists,
    node_states,
    node_pre,
    edge_states,
    edge_pre,
    node_cotangent,
    edge_cotangent,
    own_a,
    own_b,
    own_c,
    own_d,
    edge_grads,
    node_grads,
    edge_first_grad,
    edge_second_grad,
    node_first_grad,
    node_second_grad,
    all_a,
    all_b,
    all_c,
    all_d,
    sum_b,
    sum_c,
    sum_a,
    sum_d,
    from_core,
    from_x,
    from_sub,
    outgoing,
    ghosts,
    ghost_grads,
    returned,
    gather_send,
    gather_recv,
    core_send,
    core_recv,
    x_send,
    x_recv,
    sub_send,
    sub_recv,
    halo_send,
    halo_recv,
):
    doms = all_a.shape[0]
    subs = all_a.shape[1]
    width = node_states.shape[1]
    node_rows = node_states.shape[0]
    edge_rows = edge_states.shape[0]
    ghost = outgoing.shape[1]
    dom = lax.axis_index("dom")
    sub = lax.axis_index("sub")
    x_mate = lax.rem(dom + 2, doms)
    core_mate = dom + 1 - 2 * lax.rem(dom, 2)
    far_mate = x_mate + 1 - 2 * lax.rem(x_mate, 2)

    def before(step):
        return lax.rem(sub + subs - step, subs)

    def after(step):
        return lax.rem(sub + step, subs)

    barrier = pltpu.get_barrier_semaphore()
    for step in range(1, doms):
        pl.semaphore_signal(
            barrier, inc=1, device_id={"dom": lax.rem(dom + step, doms)}, device_id_type=MESH
        )
    for step in range(1, subs):
        pl.semaphore_signal(barrier, inc=1, device_id={"sub": after(step)}, device_id_type=MESH)
    pl.semaphore_wait(barrier, doms + subs - 2)

    def remote(source, target, send, recv, device):
        return pltpu.make_async_remote_copy(
            src_ref=source,
            dst_ref=target,
            send_sem=send,
            recv_sem=recv,
            device_id=device,
            device_id_type=MESH,
        )

    owns = (own_a, own_b, own_c, own_d)
    alls = (all_a, all_b, all_c, all_d)
    pending = []

    def gather_copy(part, index, source, slot, device):
        return remote(
            source,
            alls[part].at[slot[0], slot[1]],
            gather_send.at[part, index],
            gather_recv.at[part, index],
            device,
        )

    def gather_start(part, index, source, slot, device):
        copy = gather_copy(part, index, source, slot, device)
        copy.start()
        pending.append(copy)

    def gather_wait(part, index, slot):
        place = alls[part].at[slot[0], slot[1]]
        gather_copy(part, index, place, slot, {"dom": core_mate}).wait_recv()

    def to_x(part, step, source):
        gather_start(part, subs - 1 + step, source, (dom, before(step)), {"dom": x_mate})

    def to_core(part, step, source):
        gather_start(part, 2 * subs - 1 + step, source, (dom, before(step)), {"dom": core_mate})

    def gather_first(part):
        for step in range(1, subs):
            gather_start(part, step - 1, owns[part], (dom, sub), {"sub": after(step)})
        to_x(part, 0, owns[part])
        to_core(part, 0, owns[part])

    def gather_from_sub(part):
        for step in range(1, subs):
            slot = (dom, before(step))
            gather_wait(part, step - 1, slot)
            to_x(part, step, alls[part].at[slot[0], slot[1]])
            to_core(part, step, alls[part].at[slot[0], slot[1]])

    def gather_from_x(part):
        for step in range(subs):
            slot = (x_mate, before(step))
            gather_wait(part, subs - 1 + step, slot)
            gather_start(
                part,
                3 * subs - 1 + step,
                alls[part].at[slot[0], slot[1]],
                slot,
                {"dom": core_mate},
            )

    def gather_from_core(part):
        for step in range(subs):
            gather_wait(part, 2 * subs - 1 + step, (core_mate, before(step)))
            gather_wait(part, 3 * subs - 1 + step, (far_mate, before(step)))

    sums = (sum_b, sum_c, sum_a, sum_d)
    results = (node_second_grad, node_first_grad, edge_second_grad, edge_first_grad)
    units = [
        (which, first)
        for which in range(4)
        for first in range(0, sums[which].shape[2], UNIT)
    ]

    def unit_rows(unit, which_dom):
        which, first = units[unit]
        return sums[which].at[which_dom, :, pl.ds(first, UNIT), :]

    def core_copies(unit):
        return [
            remote(
                unit_rows(unit, target),
                from_core.at[unit, index],
                core_send.at[unit, index],
                core_recv.at[unit, index],
                {"dom": core_mate},
            )
            for index, target in enumerate((far_mate, core_mate))
        ]

    def x_copy(unit):
        return remote(
            unit_rows(unit, x_mate),
            from_x.at[unit],
            x_send.at[unit],
            x_recv.at[unit],
            {"dom": x_mate},
        )

    def sub_copies(unit):
        which, first = units[unit]
        return [
            remote(
                sums[which].at[dom, after(step), pl.ds(first, UNIT), :],
                from_sub.at[unit, step - 1],
                sub_send.at[unit, step - 1],
                sub_recv.at[unit, step - 1],
                {"sub": after(step)},
            )
            for step in range(1, subs)
        ]

    def reduce_core(unit):
        for copy in core_copies(unit):
            copy.start()

    def reduce_x(unit):
        far, near = core_copies(unit)
        far.wait_recv()
        rows = unit_rows(unit, x_mate)
        rows[...] = rows[...] + from_core[unit, 0]
        x_copy(unit).start()
        near.wait_recv()
        rows = unit_rows(unit, dom)
        rows[...] = rows[...] + from_core[unit, 1]

    def reduce_sub(unit):
        x_copy(unit).wait_recv()
        rows = unit_rows(unit, dom)
        rows[...] = rows[...] + from_x[unit]
        for copy in sub_copies(unit):
            copy.start()

    def reduce_last(unit):
        which, first = units[unit]
        total = sums[which][dom, sub, pl.ds(first, UNIT), :]
        for step, copy in enumerate(sub_copies(unit)):
            copy.wait_recv()
            total = total + from_sub[unit, step]
        results[which][pl.ds(first, UNIT), :] = total

    def halo_copies(source, target, turn):
        ways = (
            {"dom": lax.rem(dom + 1, doms)},
            {"dom": lax.rem(dom + doms - 1, doms)},
            {"sub": after(1)},
            {"sub": before(1)},
        )
        return [
            remote(
                source.at[index],
                target.at[index],
                halo_send.at[turn, index],
                halo_recv.at[turn, index],
                ways[index + (1 - 2 * (index % 2)) * turn],
            )
            for index in range(4)
        ]

    for part in range(4):
        gather_first(part)
    for part in range(4):
        alls[part][dom, sub] = owns[part][...]

    states = split(node_states[...])
    list_picks, list_back = picks_of(lists[...], node_rows)
    outgoing[...] = picked(list_back, states).reshape(4, ghost, width)
    ghost_copies = halo_copies(outgoing, ghosts, 0)
    for copy in ghost_copies:
        copy.start()
    target_picks, target_back = picks_of(endpoints[1:2, :], node_rows)
    source_picks, source_back = picks_of(endpoints[0:1, :], node_rows)
    ghost_picks, ghost_back = picks_of(endpoints[0:1, :], 4 * ghost, node_rows)
    live_nodes = jnp.where(
        lax.broadcasted_iota(jnp.int32, (node_rows, 1), 0) < counts[0], 1.0, 0.0
    ).astype(jnp.float32)
    live_edges = jnp.where(
        lax.broadcasted_iota(jnp.int32, (edge_rows, 1), 0) < blocks[0] * 128, 1.0, 0.0
    ).astype(jnp.float32)
    edge_act = split(jnp.maximum(edge_pre[...], 0.0))
    node_act = split(jnp.maximum(node_pre[...], 0.0))

    gather_from_sub(0)
    gather_from_sub(1)
    gather_from_x(0)
    gather_from_sub(2)
    gather_from_x(1)
    gather_from_core(0)
    second_rows = width // (doms * subs)
    edge_second = split(all_a[:, :, :second_rows, :].reshape(width, width))
    params = jnp.sum(
        all_a[:, :, second_rows:, :].reshape(doms * subs, -1, width), axis=0
    )
    edge_bias, edge_gain, edge_shift, node_bias, node_gain = (
        params[row : row + 1, :] for row in range(5)
    )
    edge_normed, edge_inverse = layer_norm(wide(edge_act, edge_second, (1, 0)) + edge_bias)
    message = (edge_normed * edge_gain + edge_shift) * live_edges
    aggregate = split(picked(target_picks, split(message)))

    gather_from_sub(3)
    gather_from_x(2)
    gather_from_core(1)
    node_second = split(all_b[...].reshape(width, width))
    node_normed, node_inverse = layer_norm(wide(node_act, node_second, (1, 0)) + node_bias)
    node_upstream = node_cotangent[...] * live_nodes
    node_grad_z = split(norm_back(node_upstream * node_gain, node_normed, node_inverse))
    sum_b[...] = (wide(node_act, node_grad_z, (0, 0)) * node_scale).reshape(sum_b.shape)
    reduce_core(0)
    node_grad_pre = split(
        wide(node_grad_z, node_second, (1, 1)) * (node_pre[...] > 0).astype(jnp.float32)
    )
    sum_c[: doms // 2] = (wide(states, node_grad_pre, (0, 0)) * node_scale).reshape(
        doms // 2, *sum_c.shape[1:]
    )
    sum_c[doms // 2 :] = (wide(aggregate, node_grad_pre, (0, 0)) * node_scale).reshape(
        doms // 2, *sum_c.shape[1:]
    )
    reduce_core(1)
    reduce_core(2)

    gather_from_x(3)
    gather_from_core(2)
    for unit in range(3):
        reduce_x(unit)
    node_first = split(all_c[...].reshape(2 * width, width))
    from_nodes = wide(
        node_grad_pre, tuple(half[width:] for half in node_first), (1, 1)
    )
    edge_upstream = (edge_cotangent[...] + picked(target_back, split(from_nodes))) * live_edges
    edge_grad_z = split(norm_back(edge_upstream * edge_gain, edge_normed, edge_inverse))
    sum_a[...] = (wide(edge_act, edge_grad_z, (0, 0)) * edge_scale).reshape(sum_a.shape)
    reduce_core(3)
    edge_grad_pre = split(
        wide(edge_grad_z, edge_second, (1, 1)) * (edge_pre[...] > 0).astype(jnp.float32)
    )
    for copy in ghost_copies:
        copy.wait_recv()
    sender = picked(source_back, states) + picked(
        ghost_back, split(ghosts[...].reshape(4 * ghost, width))
    )
    receiver = picked(target_back, states)
    first_grad = jnp.concatenate(
        [
            wide(split(feature), edge_grad_pre, (0, 0)) * edge_scale
            for feature in (edge_states[...], sender, receiver)
        ],
        axis=0,
    )
    sum_d[...] = first_grad.reshape(sum_d.shape)
    for unit in range(4, len(units)):
        reduce_core(unit)
    for unit in range(3):
        reduce_sub(unit)
    state_grads = node_upstream + wide(
        node_grad_pre, tuple(half[:width] for half in node_first), (1, 1)
    )
    for unit in range(3, len(units)):
        reduce_x(unit)

    gather_from_core(3)
    edge_first = split(all_d[...].reshape(3 * width, width))

    def edge_part(index):
        rows = slice(index * width, (index + 1) * width)
        return wide(edge_grad_pre, tuple(half[rows] for half in edge_first), (1, 1))

    sender_grads = split(edge_part(1))
    ghost_grads[...] = picked(ghost_picks, sender_grads).reshape(4, ghost, width)
    return_copies = halo_copies(ghost_grads, returned, 1)
    for copy in return_copies:
        copy.start()
    for unit in range(3, 5):
        reduce_sub(unit)
    edge_grads[...] = (edge_cotangent[...] + edge_part(0)) * live_edges
    state_grads = state_grads + picked(source_picks, sender_grads)
    state_grads = state_grads + picked(target_picks, split(edge_part(2)))
    for unit in range(5, len(units)):
        reduce_sub(unit)
    for copy in return_copies:
        copy.wait_recv()
    node_grads[...] = state_grads + picked(
        list_picks, split(returned[...].reshape(4 * ghost, width))
    )
    for unit in range(len(units)):
        reduce_last(unit)

    for copy in pending + ghost_copies + return_copies:
        copy.wait_send()
    for unit in range(len(units)):
        for copy in core_copies(unit) + [x_copy(unit)] + sub_copies(unit):
            copy.wait_send()


def kernel_shards(
    node_states,
    node_pre,
    edge_states,
    edge_pre,
    node_cotangent,
    edge_cotangent,
    endpoints,
    send_lists,
    node_counts,
    edge_blocks,
    edge_first,
    edge_second,
    edge_bias,
    edge_gain,
    edge_shift,
    node_first,
    node_second,
    node_bias,
    node_gain,
):
    node_rows, width = node_states.shape
    edge_rows = edge_states.shape[0]
    ghost = send_lists.shape[2]
    doms, subs = lax.axis_size("dom"), lax.axis_size("sub")
    peers = doms * subs
    mine = lax.axis_index("dom") * subs + lax.axis_index("sub")
    place = jnp.arange(width) // (width // peers) == mine
    vectors = jnp.stack([edge_bias, edge_gain, edge_shift, node_bias, node_gain])
    spread = jnp.where(place[None, :], jnp.tile(vectors, (1, peers)), 0.0)
    own_a = jnp.concatenate([edge_second, spread, jnp.zeros((3, width), jnp.float32)], axis=0)
    owns = (own_a, node_second, node_first, edge_first)
    sums = (node_second, node_first, edge_second, edge_first)
    units = sum(shard.shape[0] for shard in sums) // UNIT
    vmem = pl.BlockSpec(memory_space=pltpu.VMEM)
    smem = pl.BlockSpec(memory_space=pltpu.SMEM)
    f32 = jnp.float32
    dma = pltpu.SemaphoreType.DMA
    halo = pltpu.VMEM((4, ghost, width), f32)
    return pl.pallas_call(
        functools.partial(
            layer_kernel,
            1.0 / math.sqrt(edge_rows * peers),
            1.0 / math.sqrt(node_rows * peers),
        ),
        out_shape=[
            jax.ShapeDtypeStruct(shape, f32)
            for shape in (
                edge_states.shape,
                node_states.shape,
                edge_first.shape,
                edge_second.shape,
                node_first.shape,
                node_second.shape,
            )
        ],
        in_specs=[smem, smem] + [vmem] * 12,
        out_specs=[vmem] * 6,
        scratch_shapes=[pltpu.VMEM((doms, subs) + own.shape, f32) for own in owns]
        + [pltpu.VMEM((doms, subs) + shard.shape, f32) for shard in sums]
        + [
            pltpu.VMEM((units, 2, subs, UNIT, width), f32),
            pltpu.VMEM((units, subs, UNIT, width), f32),
            pltpu.VMEM((units, subs - 1, UNIT, width), f32),
            halo,
            halo,
            halo,
            halo,
            dma((4, 4 * subs - 1)),
            dma((4, 4 * subs - 1)),
            dma((units, 2)),
            dma((units, 2)),
            dma((units,)),
            dma((units,)),
            dma((units, subs - 1)),
            dma((units, subs - 1)),
            dma((2, 4)),
            dma((2, 4)),
        ],
        compiler_params=pltpu.CompilerParams(
            collective_id=0, has_side_effects=True, vmem_limit_bytes=56 * 2**20
        ),
    )(
        node_counts,
        edge_blocks,
        endpoints,
        send_lists.reshape(1, 4 * ghost),
        node_states,
        node_pre,
        edge_states,
        edge_pre,
        node_cotangent,
        edge_cotangent,
        *owns,
    )


def shards(*blocks):
    weights = (blocks[10], blocks[11], blocks[15], blocks[16])
    fits = all(weight.shape[0] % UNIT == 0 for weight in weights)
    if lax.axis_size("dom") == 4 and lax.axis_size("sub") > 2 and fits:
        return tuple(kernel_shards(*blocks))
    return plain_shards(*blocks)


def solution(mesh):
    in_specs = (
        P(("groups", "dom", "sub"), None),
        P(("groups", "dom", "sub"), None),
        P(("groups", "dom", "sub"), None),
        P(("groups", "dom", "sub"), None),
        P(("groups", "dom", "sub"), None),
        P(("groups", "dom", "sub"), None),
        P(None, ("groups", "dom", "sub")),
        P(("groups", "dom", "sub"), None, None),
        P(("groups", "dom", "sub")),
        P(("groups", "dom", "sub")),
        P(("dom", "sub"), None),
        P(("dom", "sub"), None),
        P(("dom", "sub")),
        P(("dom", "sub")),
        P(("dom", "sub")),
        P(("dom", "sub"), None),
        P(("dom", "sub"), None),
        P(("dom", "sub")),
        P(("dom", "sub")),
    )
    out_specs = (
        P(("groups", "dom", "sub"), None),
        P(("groups", "dom", "sub"), None),
        P(("groups", "dom", "sub"), None),
        P(("groups", "dom", "sub"), None),
        P(("groups", "dom", "sub"), None),
        P(("groups", "dom", "sub"), None),
    )
    return jax.shard_map(shards, mesh=mesh, in_specs=in_specs, out_specs=out_specs, check_vma=False)
```

```python
import functools
import math

import jax
import jax.numpy as jnp
from jax import lax
from jax.experimental import pallas as pl
from jax.experimental.pallas import tpu as pltpu
from jax.sharding import PartitionSpec as P

EPSILON = 1e-05


def padded(cells, sides, width):
    for axis, dim in sides:
        count = lax.axis_size(axis)
        ends = count - 1
        head = lax.slice_in_dim(cells, 0, width, axis=dim)
        tail = lax.slice_in_dim(cells, cells.shape[dim] - width, cells.shape[dim], axis=dim)
        cells = jnp.concatenate(
            [
                lax.ppermute(tail, axis, [(i, (i + 1) % count) for i in range(ends)]),
                cells,
                lax.ppermute(head, axis, [((i + 1) % count, i) for i in range(ends)]),
            ],
            axis=dim,
        )
    return cells


def matmul(left, right):
    return jnp.dot(left, right, precision=lax.Precision.HIGHEST, preferred_element_type=jnp.float32)


def inner(left, right):
    return lax.dot_general(
        left,
        right,
        (((0,), (0,)), ((), ())),
        precision=lax.Precision.HIGHEST,
        preferred_element_type=jnp.float32,
    )


def outer_back(left, right):
    return lax.dot_general(
        left,
        right,
        (((1,), (1,)), ((), ())),
        precision=lax.Precision.HIGHEST,
        preferred_element_type=jnp.float32,
    )


def layer_norm(values):
    center = values - jnp.mean(values, axis=-1, keepdims=True)
    inverse = 1.0 / jnp.sqrt(jnp.mean(center * center, axis=-1, keepdims=True) + EPSILON)
    return (center * inverse, inverse)


def norm_back(upstream, normed, inverse):
    first = jnp.mean(upstream, axis=-1, keepdims=True)
    second = jnp.mean(upstream * normed, axis=-1, keepdims=True)
    return inverse * (upstream - first - normed * second)


def plain_shards(
    node_states,
    node_pre,
    edge_states,
    edge_pre,
    node_cotangent,
    edge_cotangent,
    endpoints,
    send_lists,
    node_counts,
    edge_blocks,
    edge_first,
    edge_second,
    edge_bias,
    edge_gain,
    edge_shift,
    node_first,
    node_second,
    node_bias,
    node_gain,
):
    node_rows, width = node_states.shape
    edge_rows = edge_states.shape[0]
    ghost = send_lists.shape[2]
    dom_count = lax.axis_size("dom")
    sub_count = lax.axis_size("sub")
    peer_count = dom_count * sub_count
    lists = send_lists[0]
    outgoing = jnp.take(node_states, lists.reshape(-1), axis=0).reshape(4, ghost, width)
    dom_side = padded(jnp.stack([outgoing[1], outgoing[0]]), (("dom", 0),), 1)
    sub_side = padded(jnp.stack([outgoing[3], outgoing[2]]), (("sub", 0),), 1)
    ghosts = jnp.stack([dom_side[0], dom_side[3], sub_side[0], sub_side[3]])
    ghosts = ghosts.reshape(4 * ghost, width)
    full_node_first, full_node_second, full_node_bias, full_node_gain = (
        lax.all_gather(node_first, ("dom", "sub"), axis=0, tiled=True),
        lax.all_gather(node_second, ("dom", "sub"), axis=0, tiled=True),
        lax.all_gather(node_bias, ("dom", "sub"), axis=0, tiled=True),
        lax.all_gather(node_gain, ("dom", "sub"), axis=0, tiled=True),
    )
    full_edge_first, full_edge_second, full_edge_bias, full_edge_gain, full_edge_shift = (
        lax.all_gather(edge_first, ("dom", "sub"), axis=0, tiled=True),
        lax.all_gather(edge_second, ("dom", "sub"), axis=0, tiled=True),
        lax.all_gather(edge_bias, ("dom", "sub"), axis=0, tiled=True),
        lax.all_gather(edge_gain, ("dom", "sub"), axis=0, tiled=True),
        lax.all_gather(edge_shift, ("dom", "sub"), axis=0, tiled=True),
    )
    live_nodes = (jnp.arange(node_rows) < node_counts[0]).astype(jnp.float32)[:, None]
    live_edges = (jnp.arange(edge_rows) < edge_blocks[0] * 128).astype(jnp.float32)[:, None]
    source = endpoints[0]
    target = endpoints[1]
    edge_scale = 1.0 / math.sqrt(edge_rows * peer_count)
    node_scale = 1.0 / math.sqrt(node_rows * peer_count)
    edge_act = jnp.maximum(edge_pre, 0.0)
    edge_normed, edge_inverse = layer_norm(matmul(edge_act, full_edge_second) + full_edge_bias)
    message = (edge_normed * full_edge_gain + full_edge_shift) * live_edges
    aggregate = jax.ops.segment_sum(message, target, node_rows)
    node_act = jnp.maximum(node_pre, 0.0)
    node_normed, node_inverse = layer_norm(matmul(node_act, full_node_second) + full_node_bias)
    node_upstream = node_cotangent * live_nodes
    node_grad_z = norm_back(node_upstream * full_node_gain, node_normed, node_inverse)
    node_grad_pre = outer_back(node_grad_z, full_node_second) * (node_pre > 0).astype(jnp.float32)
    node_input = jnp.concatenate([node_states, aggregate], axis=1)
    node_first_grad, node_second_grad = (
        lax.psum_scatter(
            inner(node_input, node_grad_pre) * node_scale,
            ("dom", "sub"),
            scatter_dimension=0,
            tiled=True,
        ),
        lax.psum_scatter(
            inner(node_act, node_grad_z) * node_scale,
            ("dom", "sub"),
            scatter_dimension=0,
            tiled=True,
        ),
    )
    node_grad_input = outer_back(node_grad_pre, full_node_first)
    state_grads = node_upstream + node_grad_input[:, :width]
    edge_upstream = (
        edge_cotangent + jnp.take(node_grad_input[:, width:], target, axis=0)
    ) * live_edges
    edge_grad_z = norm_back(edge_upstream * full_edge_gain, edge_normed, edge_inverse)
    edge_grad_pre = outer_back(edge_grad_z, full_edge_second) * (edge_pre > 0).astype(jnp.float32)
    edge_second_grad = lax.psum_scatter(
        inner(edge_act, edge_grad_z) * edge_scale, ("dom", "sub"), scatter_dimension=0, tiled=True
    )
    extended = jnp.concatenate([node_states, ghosts], axis=0)
    features = jnp.concatenate(
        [edge_states, jnp.take(extended, source, axis=0), jnp.take(extended, target, axis=0)],
        axis=1,
    )
    edge_first_grad = lax.psum_scatter(
        inner(features, edge_grad_pre) * edge_scale, ("dom", "sub"), scatter_dimension=0, tiled=True
    )
    edge_grad_input = outer_back(edge_grad_pre, full_edge_first)
    edge_grads = (edge_cotangent + edge_grad_input[:, :width]) * live_edges
    extended_grads = jax.ops.segment_sum(
        edge_grad_input[:, width : 2 * width], source, node_rows + 4 * ghost
    )
    extended_grads = extended_grads + jax.ops.segment_sum(
        edge_grad_input[:, 2 * width :], target, node_rows + 4 * ghost
    )
    state_grads = state_grads + extended_grads[:node_rows]
    ghost_grads = extended_grads[node_rows:].reshape(4, ghost, width)
    dom_back = padded(jnp.stack([ghost_grads[0], ghost_grads[1]]), (("dom", 0),), 1)
    sub_back = padded(jnp.stack([ghost_grads[2], ghost_grads[3]]), (("sub", 0),), 1)
    returned = jnp.stack([dom_back[3], dom_back[0], sub_back[3], sub_back[0]])
    state_grads = state_grads + jax.ops.segment_sum(
        returned.reshape(-1, width), lists.reshape(-1), node_rows
    )
    return (
        edge_grads,
        state_grads,
        edge_first_grad,
        edge_second_grad,
        node_first_grad,
        node_second_grad,
    )


MESH = pl.DeviceIdType.MESH
UNIT = 32


def split(values):
    high = values.astype(jnp.bfloat16)
    return (high, (values - high.astype(jnp.float32)).astype(jnp.bfloat16))


def product(left, right, dims):
    return lax.dot_general(
        left, right, ((dims[:1], dims[1:]), ((), ())), preferred_element_type=jnp.float32
    )


def wide(left, right, dims):
    return (
        product(left[0], right[1], dims)
        + product(left[1], right[0], dims)
        + product(left[0], right[0], dims)
    )


def picked(picks, right, dims=(1, 0)):
    return product(picks, right[1], dims) + product(picks, right[0], dims)


def picks_of(slots, rows, first=0):
    place = lax.broadcasted_iota(jnp.int32, (rows, slots.shape[1]), 0) + first
    ones = jnp.where(place == slots, 1.0, 0.0).astype(jnp.float32)
    return (ones.astype(jnp.bfloat16), ones.T.astype(jnp.bfloat16))


def layer_kernel(
    edge_scale,
    node_scale,
    counts,
    blocks,
    endpoints,
    lists,
    node_states,
    node_pre,
    edge_states,
    edge_pre,
    node_cotangent,
    edge_cotangent,
    own_a,
    own_b,
    own_c,
    own_d,
    edge_grads,
    node_grads,
    edge_first_grad,
    edge_second_grad,
    node_first_grad,
    node_second_grad,
    all_a,
    all_b,
    all_c,
    all_d,
    sum_b,
    sum_c,
    sum_a,
    sum_d,
    from_core,
    from_x,
    from_sub,
    outgoing,
    ghosts,
    ghost_grads,
    returned,
    gather_send,
    gather_recv,
    core_send,
    core_recv,
    x_send,
    x_recv,
    sub_send,
    sub_recv,
    halo_send,
    halo_recv,
):
    doms = all_a.shape[0]
    subs = all_a.shape[1]
    width = node_states.shape[1]
    node_rows = node_states.shape[0]
    edge_rows = edge_states.shape[0]
    ghost = outgoing.shape[1]
    dom = lax.axis_index("dom")
    sub = lax.axis_index("sub")
    group = lax.axis_index("groups")
    x_mate = lax.rem(dom + 2, doms)
    core_mate = dom + 1 - 2 * lax.rem(dom, 2)
    far_mate = x_mate + 1 - 2 * lax.rem(x_mate, 2)

    def before(step):
        return lax.rem(sub + subs - step, subs)

    def after(step):
        return lax.rem(sub + step, subs)

    barrier = pltpu.get_barrier_semaphore()
    for step in range(1, doms):
        pl.semaphore_signal(
            barrier, inc=1, device_id={"dom": lax.rem(dom + step, doms)}, device_id_type=MESH
        )
    for step in range(1, subs):
        pl.semaphore_signal(barrier, inc=1, device_id={"sub": after(step)}, device_id_type=MESH)
    pl.semaphore_signal(barrier, inc=1, device_id={"groups": 1 - group}, device_id_type=MESH)
    pl.semaphore_wait(barrier, doms + subs - 1)

    def remote(source, target, send, recv, device):
        return pltpu.make_async_remote_copy(
            src_ref=source,
            dst_ref=target,
            send_sem=send,
            recv_sem=recv,
            device_id=device,
            device_id_type=MESH,
        )

    owns = (own_a, own_b, own_c, own_d)
    alls = (all_a, all_b, all_c, all_d)
    shared = (False, False, True, True)
    pending = []

    def rows_of(ref, part, half):
        if half is None or not shared[part]:
            return ref
        count = owns[part].shape[0] // 2
        return ref.at[pl.ds(pl.multiple_of(half * count, 16), count), :]

    def place_of(part, slot, half):
        return rows_of(alls[part].at[slot[0], slot[1]], part, half)

    def gather_copy(part, index, source, target, device):
        return remote(
            source, target, gather_send.at[part, index], gather_recv.at[part, index], device
        )

    def gather_start(part, index, slot, half, device, own=False):
        target = place_of(part, slot, half)
        source = rows_of(owns[part], part, half) if own else target
        copy = gather_copy(part, index, source, target, device)
        copy.start()
        pending.append(copy)

    def gather_wait(part, index, slot, half):
        place = place_of(part, slot, half)
        gather_copy(part, index, place, place, {"dom": core_mate}).wait_recv()

    SUB, X = 0, subs - 1
    CORE_NEAR, CORE_FAR = 2 * subs - 1, 3 * subs - 1
    Y_NEAR, Y_FAR = 4 * subs - 1, 5 * subs - 1
    LATE_NEAR, LATE_FAR = 6 * subs - 1, 7 * subs - 1
    to_x, to_core, to_y = {"dom": x_mate}, {"dom": core_mate}, {"groups": 1 - group}

    def gather_first(part):
        for step in range(1, subs):
            gather_start(part, SUB + step - 1, (dom, sub), group, {"sub": after(step)}, True)
        gather_start(part, X, (dom, sub), group, to_x, True)
        gather_start(part, CORE_NEAR, (dom, sub), None, to_core, True)

    def gather_from_sub(part, steps=range(1, subs)):
        for step in steps:
            slot = (dom, before(step))
            gather_wait(part, SUB + step - 1, slot, group)
            gather_start(part, X + step, slot, group, to_x)
            if shared[part]:
                gather_start(part, Y_NEAR + step, slot, group, to_y)
            gather_start(part, CORE_NEAR + step, slot, group, to_core)

    def gather_from_x(part):
        for step in range(subs):
            slot = (x_mate, before(step))
            gather_wait(part, X + step, slot, group)
            if shared[part]:
                gather_start(part, Y_FAR + step, slot, group, to_y)
            gather_start(part, CORE_FAR + step, slot, group, to_core)

    def gather_from_y(part):
        for step in range(1, subs):
            slot = (dom, before(step))
            gather_wait(part, Y_NEAR + step, slot, 1 - group)
            gather_start(part, LATE_NEAR + step, slot, 1 - group, to_core)
        for step in range(subs):
            slot = (x_mate, before(step))
            gather_wait(part, Y_FAR + step, slot, 1 - group)
            gather_start(part, LATE_FAR + step, slot, 1 - group, to_core)

    def gather_from_core(part):
        for step in range(subs):
            near, far = (core_mate, before(step)), (far_mate, before(step))
            gather_wait(part, CORE_NEAR + step, near, group if step else None)
            gather_wait(part, CORE_FAR + step, far, group)
            if shared[part]:
                if step:
                    gather_wait(part, LATE_NEAR + step, near, 1 - group)
                gather_wait(part, LATE_FAR + step, far, 1 - group)

    sums = (sum_b, sum_c, sum_a, sum_d)
    results = (node_second_grad, node_first_grad, edge_second_grad, edge_first_grad)
    units = [
        (which, first)
        for which in range(4)
        for first in range(0, sums[which].shape[2], UNIT)
    ]

    def unit_rows(unit, which_dom):
        which, first = units[unit]
        return sums[which].at[which_dom, :, pl.ds(first, UNIT), :]

    def core_copies(unit):
        return [
            remote(
                unit_rows(unit, target),
                from_core.at[unit, index],
                core_send.at[unit, index],
                core_recv.at[unit, index],
                {"dom": core_mate},
            )
            for index, target in enumerate((far_mate, core_mate))
        ]

    def x_copy(unit):
        return remote(
            unit_rows(unit, x_mate),
            from_x.at[unit],
            x_send.at[unit],
            x_recv.at[unit],
            {"dom": x_mate},
        )

    def sub_copies(unit):
        which, first = units[unit]
        return [
            remote(
                sums[which].at[dom, after(step), pl.ds(first, UNIT), :],
                from_sub.at[unit, step - 1],
                sub_send.at[unit, step - 1],
                sub_recv.at[unit, step - 1],
                {"sub": after(step)},
            )
            for step in range(1, subs)
        ]

    def reduce_core(unit):
        for copy in core_copies(unit):
            copy.start()

    def reduce_x(unit):
        far, near = core_copies(unit)
        far.wait_recv()
        rows = unit_rows(unit, x_mate)
        rows[...] = rows[...] + from_core[unit, 0]
        x_copy(unit).start()
        near.wait_recv()
        rows = unit_rows(unit, dom)
        rows[...] = rows[...] + from_core[unit, 1]

    def reduce_sub(unit):
        x_copy(unit).wait_recv()
        rows = unit_rows(unit, dom)
        rows[...] = rows[...] + from_x[unit]
        for copy in sub_copies(unit):
            copy.start()

    def reduce_last(unit):
        which, first = units[unit]
        total = sums[which][dom, sub, pl.ds(first, UNIT), :]
        for step, copy in enumerate(sub_copies(unit)):
            copy.wait_recv()
            total = total + from_sub[unit, step]
        results[which][pl.ds(first, UNIT), :] = total

    def halo_copies(source, target, turn):
        ways = (
            {"dom": lax.rem(dom + 1, doms)},
            {"dom": lax.rem(dom + doms - 1, doms)},
            {"sub": after(1)},
            {"sub": before(1)},
        )
        return [
            remote(
                source.at[index],
                target.at[index],
                halo_send.at[turn, index],
                halo_recv.at[turn, index],
                ways[index + (1 - 2 * (index % 2)) * turn],
            )
            for index in range(4)
        ]

    for part in range(2):
        gather_first(part)
    for part in range(4):
        alls[part][dom, sub] = owns[part][...]

    states = split(node_states[...])
    list_picks, list_back = picks_of(lists[...], node_rows)
    outgoing[...] = picked(list_back, states).reshape(4, ghost, width)
    ghost_copies = halo_copies(outgoing, ghosts, 0)
    for copy in ghost_copies:
        copy.start()
    target_picks, target_back = picks_of(endpoints[1:2, :], node_rows)
    source_picks, source_back = picks_of(endpoints[0:1, :], node_rows)
    ghost_picks, ghost_back = picks_of(endpoints[0:1, :], 4 * ghost, node_rows)
    live_nodes = jnp.where(
        lax.broadcasted_iota(jnp.int32, (node_rows, 1), 0) < counts[0], 1.0, 0.0
    ).astype(jnp.float32)
    live_edges = jnp.where(
        lax.broadcasted_iota(jnp.int32, (edge_rows, 1), 0) < blocks[0] * 128, 1.0, 0.0
    ).astype(jnp.float32)
    edge_act = split(jnp.maximum(edge_pre[...], 0.0))
    node_act = split(jnp.maximum(node_pre[...], 0.0))

    gather_from_sub(0)
    gather_first(2)
    gather_from_sub(1)
    gather_from_x(0)
    gather_from_x(1)
    gather_from_core(0)
    second_rows = width // (doms * subs)
    edge_second = split(all_a[:, :, :second_rows, :].reshape(width, width))
    params = jnp.sum(
        all_a[:, :, second_rows:, :].reshape(doms * subs, -1, width), axis=0
    )
    edge_bias, edge_gain, edge_shift, node_bias, node_gain = (
        params[row : row + 1, :] for row in range(5)
    )
    edge_normed, edge_inverse = layer_norm(wide(edge_act, edge_second, (1, 0)) + edge_bias)
    message = (edge_normed * edge_gain + edge_shift) * live_edges
    aggregate = split(picked(target_picks, split(message)))

    gather_from_sub(2, [1])
    gather_from_core(1)
    node_second = split(all_b[...].reshape(width, width))
    node_normed, node_inverse = layer_norm(wide(node_act, node_second, (1, 0)) + node_bias)
    gather_from_sub(2, range(2, subs))
    gather_first(3)
    node_upstream = node_cotangent[...] * live_nodes
    node_grad_z = split(norm_back(node_upstream * node_gain, node_normed, node_inverse))
    gather_from_x(2)
    sum_b[...] = (wide(node_act, node_grad_z, (0, 0)) * node_scale).reshape(sum_b.shape)
    reduce_core(0)
    node_grad_pre = split(
        wide(node_grad_z, node_second, (1, 1)) * (node_pre[...] > 0).astype(jnp.float32)
    )
    gather_from_y(2)
    sum_c[: doms // 2] = (wide(states, node_grad_pre, (0, 0)) * node_scale).reshape(
        doms // 2, *sum_c.shape[1:]
    )
    sum_c[doms // 2 :] = (wide(aggregate, node_grad_pre, (0, 0)) * node_scale).reshape(
        doms // 2, *sum_c.shape[1:]
    )
    reduce_core(1)
    reduce_core(2)

    gather_from_sub(3, range(1, subs - 1))
    reduce_x(0)
    gather_from_core(2)
    reduce_x(1)
    reduce_x(2)
    node_first = split(all_c[...].reshape(2 * width, width))
    from_nodes = wide(
        node_grad_pre, tuple(half[width:] for half in node_first), (1, 1)
    )
    edge_upstream = (edge_cotangent[...] + picked(target_back, split(from_nodes))) * live_edges
    edge_grad_z = split(norm_back(edge_upstream * edge_gain, edge_normed, edge_inverse))
    gather_from_sub(3, [subs - 1])
    sum_a[...] = (wide(edge_act, edge_grad_z, (0, 0)) * edge_scale).reshape(sum_a.shape)
    reduce_core(3)
    edge_grad_pre = split(
        wide(edge_grad_z, edge_second, (1, 1)) * (edge_pre[...] > 0).astype(jnp.float32)
    )
    gather_from_x(3)
    reduce_sub(0)
    for copy in ghost_copies:
        copy.wait_recv()
    sender = picked(source_back, states) + picked(
        ghost_back, split(ghosts[...].reshape(4 * ghost, width))
    )
    receiver = picked(target_back, states)
    first_grad = jnp.concatenate(
        [
            wide(split(feature), edge_grad_pre, (0, 0)) * edge_scale
            for feature in (edge_states[...], sender, receiver)
        ],
        axis=0,
    )
    sum_d[...] = first_grad.reshape(sum_d.shape)
    for unit in range(4, len(units)):
        reduce_core(unit)
    reduce_x(3)
    reduce_sub(1)
    reduce_sub(2)
    gather_from_y(3)
    for unit in range(4, len(units)):
        reduce_x(unit)
    state_grads = node_upstream + wide(
        node_grad_pre, tuple(half[:width] for half in node_first), (1, 1)
    )

    gather_from_core(3)
    edge_first = split(all_d[...].reshape(3 * width, width))

    def edge_part(index):
        rows = slice(index * width, (index + 1) * width)
        return wide(edge_grad_pre, tuple(half[rows] for half in edge_first), (1, 1))

    sender_grads = split(edge_part(1))
    ghost_grads[...] = picked(ghost_picks, sender_grads).reshape(4, ghost, width)
    return_copies = halo_copies(ghost_grads, returned, 1)
    for copy in return_copies:
        copy.start()
    for unit in range(3, 5):
        reduce_sub(unit)
    edge_grads[...] = (edge_cotangent[...] + edge_part(0)) * live_edges
    state_grads = state_grads + picked(source_picks, sender_grads)
    state_grads = state_grads + picked(target_picks, split(edge_part(2)))
    for unit in range(5, len(units)):
        reduce_sub(unit)
    for copy in return_copies:
        copy.wait_recv()
    node_grads[...] = state_grads + picked(
        list_picks, split(returned[...].reshape(4 * ghost, width))
    )
    for unit in range(len(units)):
        reduce_last(unit)

    for copy in pending + ghost_copies + return_copies:
        copy.wait_send()
    for unit in range(len(units)):
        for copy in core_copies(unit) + [x_copy(unit)] + sub_copies(unit):
            copy.wait_send()


def kernel_shards(
    node_states,
    node_pre,
    edge_states,
    edge_pre,
    node_cotangent,
    edge_cotangent,
    endpoints,
    send_lists,
    node_counts,
    edge_blocks,
    edge_first,
    edge_second,
    edge_bias,
    edge_gain,
    edge_shift,
    node_first,
    node_second,
    node_bias,
    node_gain,
):
    node_rows, width = node_states.shape
    edge_rows = edge_states.shape[0]
    ghost = send_lists.shape[2]
    doms, subs = lax.axis_size("dom"), lax.axis_size("sub")
    peers = doms * subs
    mine = lax.axis_index("dom") * subs + lax.axis_index("sub")
    place = jnp.arange(width) // (width // peers) == mine
    vectors = jnp.stack([edge_bias, edge_gain, edge_shift, node_bias, node_gain])
    spread = jnp.where(place[None, :], jnp.tile(vectors, (1, peers)), 0.0)
    own_a = jnp.concatenate([edge_second, spread, jnp.zeros((3, width), jnp.float32)], axis=0)
    owns = (own_a, node_second, node_first, edge_first)
    sums = (node_second, node_first, edge_second, edge_first)
    units = sum(shard.shape[0] for shard in sums) // UNIT
    vmem = pl.BlockSpec(memory_space=pltpu.VMEM)
    smem = pl.BlockSpec(memory_space=pltpu.SMEM)
    f32 = jnp.float32
    dma = pltpu.SemaphoreType.DMA
    halo = pltpu.VMEM((4, ghost, width), f32)
    return pl.pallas_call(
        functools.partial(
            layer_kernel,
            1.0 / math.sqrt(edge_rows * peers),
            1.0 / math.sqrt(node_rows * peers),
        ),
        out_shape=[
            jax.ShapeDtypeStruct(shape, f32)
            for shape in (
                edge_states.shape,
                node_states.shape,
                edge_first.shape,
                edge_second.shape,
                node_first.shape,
                node_second.shape,
            )
        ],
        in_specs=[smem, smem] + [vmem] * 12,
        out_specs=[vmem] * 6,
        scratch_shapes=[pltpu.VMEM((doms, subs) + own.shape, f32) for own in owns]
        + [pltpu.VMEM((doms, subs) + shard.shape, f32) for shard in sums]
        + [
            pltpu.VMEM((units, 2, subs, UNIT, width), f32),
            pltpu.VMEM((units, subs, UNIT, width), f32),
            pltpu.VMEM((units, subs - 1, UNIT, width), f32),
            halo,
            halo,
            halo,
            halo,
            dma((4, 8 * subs - 1)),
            dma((4, 8 * subs - 1)),
            dma((units, 2)),
            dma((units, 2)),
            dma((units,)),
            dma((units,)),
            dma((units, subs - 1)),
            dma((units, subs - 1)),
            dma((2, 4)),
            dma((2, 4)),
        ],
        compiler_params=pltpu.CompilerParams(
            collective_id=0, has_side_effects=True, vmem_limit_bytes=56 * 2**20
        ),
    )(
        node_counts,
        edge_blocks,
        endpoints,
        send_lists.reshape(1, 4 * ghost),
        node_states,
        node_pre,
        edge_states,
        edge_pre,
        node_cotangent,
        edge_cotangent,
        *owns,
    )


def shards(*blocks):
    weights = (blocks[10], blocks[11], blocks[15], blocks[16])
    fits = all(weight.shape[0] % UNIT == 0 for weight in weights)
    paired = lax.axis_size("groups") == 2 and lax.axis_size("dom") == 4
    if paired and lax.axis_size("sub") > 2 and fits:
        return tuple(kernel_shards(*blocks))
    return plain_shards(*blocks)


def solution(mesh):
    in_specs = (
        P(("groups", "dom", "sub"), None),
        P(("groups", "dom", "sub"), None),
        P(("groups", "dom", "sub"), None),
        P(("groups", "dom", "sub"), None),
        P(("groups", "dom", "sub"), None),
        P(("groups", "dom", "sub"), None),
        P(None, ("groups", "dom", "sub")),
        P(("groups", "dom", "sub"), None, None),
        P(("groups", "dom", "sub")),
        P(("groups", "dom", "sub")),
        P(("dom", "sub"), None),
        P(("dom", "sub"), None),
        P(("dom", "sub")),
        P(("dom", "sub")),
        P(("dom", "sub")),
        P(("dom", "sub"), None),
        P(("dom", "sub"), None),
        P(("dom", "sub")),
        P(("dom", "sub")),
    )
    out_specs = (
        P(("groups", "dom", "sub"), None),
        P(("groups", "dom", "sub"), None),
        P(("groups", "dom", "sub"), None),
        P(("groups", "dom", "sub"), None),
        P(("groups", "dom", "sub"), None),
        P(("groups", "dom", "sub"), None),
    )
    return jax.shard_map(shards, mesh=mesh, in_specs=in_specs, out_specs=out_specs, check_vma=False)
```

```python
import functools
import math

import jax
import jax.numpy as jnp
from jax import lax
from jax.experimental import pallas as pl
from jax.experimental.pallas import tpu as pltpu
from jax.sharding import PartitionSpec as P

EPSILON = 1e-05


def padded(cells, sides, width):
    for axis, dim in sides:
        count = lax.axis_size(axis)
        ends = count - 1
        head = lax.slice_in_dim(cells, 0, width, axis=dim)
        tail = lax.slice_in_dim(cells, cells.shape[dim] - width, cells.shape[dim], axis=dim)
        cells = jnp.concatenate(
            [
                lax.ppermute(tail, axis, [(i, (i + 1) % count) for i in range(ends)]),
                cells,
                lax.ppermute(head, axis, [((i + 1) % count, i) for i in range(ends)]),
            ],
            axis=dim,
        )
    return cells


def matmul(left, right):
    return jnp.dot(left, right, precision=lax.Precision.HIGHEST, preferred_element_type=jnp.float32)


def inner(left, right):
    return lax.dot_general(
        left,
        right,
        (((0,), (0,)), ((), ())),
        precision=lax.Precision.HIGHEST,
        preferred_element_type=jnp.float32,
    )


def outer_back(left, right):
    return lax.dot_general(
        left,
        right,
        (((1,), (1,)), ((), ())),
        precision=lax.Precision.HIGHEST,
        preferred_element_type=jnp.float32,
    )


def layer_norm(values):
    center = values - jnp.mean(values, axis=-1, keepdims=True)
    inverse = 1.0 / jnp.sqrt(jnp.mean(center * center, axis=-1, keepdims=True) + EPSILON)
    return (center * inverse, inverse)


def norm_back(upstream, normed, inverse):
    first = jnp.mean(upstream, axis=-1, keepdims=True)
    second = jnp.mean(upstream * normed, axis=-1, keepdims=True)
    return inverse * (upstream - first - normed * second)


def plain_shards(
    node_states,
    node_pre,
    edge_states,
    edge_pre,
    node_cotangent,
    edge_cotangent,
    endpoints,
    send_lists,
    node_counts,
    edge_blocks,
    edge_first,
    edge_second,
    edge_bias,
    edge_gain,
    edge_shift,
    node_first,
    node_second,
    node_bias,
    node_gain,
):
    node_rows, width = node_states.shape
    edge_rows = edge_states.shape[0]
    ghost = send_lists.shape[2]
    dom_count = lax.axis_size("dom")
    sub_count = lax.axis_size("sub")
    peer_count = dom_count * sub_count
    lists = send_lists[0]
    outgoing = jnp.take(node_states, lists.reshape(-1), axis=0).reshape(4, ghost, width)
    dom_side = padded(jnp.stack([outgoing[1], outgoing[0]]), (("dom", 0),), 1)
    sub_side = padded(jnp.stack([outgoing[3], outgoing[2]]), (("sub", 0),), 1)
    ghosts = jnp.stack([dom_side[0], dom_side[3], sub_side[0], sub_side[3]])
    ghosts = ghosts.reshape(4 * ghost, width)
    full_node_first, full_node_second, full_node_bias, full_node_gain = (
        lax.all_gather(node_first, ("dom", "sub"), axis=0, tiled=True),
        lax.all_gather(node_second, ("dom", "sub"), axis=0, tiled=True),
        lax.all_gather(node_bias, ("dom", "sub"), axis=0, tiled=True),
        lax.all_gather(node_gain, ("dom", "sub"), axis=0, tiled=True),
    )
    full_edge_first, full_edge_second, full_edge_bias, full_edge_gain, full_edge_shift = (
        lax.all_gather(edge_first, ("dom", "sub"), axis=0, tiled=True),
        lax.all_gather(edge_second, ("dom", "sub"), axis=0, tiled=True),
        lax.all_gather(edge_bias, ("dom", "sub"), axis=0, tiled=True),
        lax.all_gather(edge_gain, ("dom", "sub"), axis=0, tiled=True),
        lax.all_gather(edge_shift, ("dom", "sub"), axis=0, tiled=True),
    )
    live_nodes = (jnp.arange(node_rows) < node_counts[0]).astype(jnp.float32)[:, None]
    live_edges = (jnp.arange(edge_rows) < edge_blocks[0] * 128).astype(jnp.float32)[:, None]
    source = endpoints[0]
    target = endpoints[1]
    edge_scale = 1.0 / math.sqrt(edge_rows * peer_count)
    node_scale = 1.0 / math.sqrt(node_rows * peer_count)
    edge_act = jnp.maximum(edge_pre, 0.0)
    edge_normed, edge_inverse = layer_norm(matmul(edge_act, full_edge_second) + full_edge_bias)
    message = (edge_normed * full_edge_gain + full_edge_shift) * live_edges
    aggregate = jax.ops.segment_sum(message, target, node_rows)
    node_act = jnp.maximum(node_pre, 0.0)
    node_normed, node_inverse = layer_norm(matmul(node_act, full_node_second) + full_node_bias)
    node_upstream = node_cotangent * live_nodes
    node_grad_z = norm_back(node_upstream * full_node_gain, node_normed, node_inverse)
    node_grad_pre = outer_back(node_grad_z, full_node_second) * (node_pre > 0).astype(jnp.float32)
    node_input = jnp.concatenate([node_states, aggregate], axis=1)
    node_first_grad, node_second_grad = (
        lax.psum_scatter(
            inner(node_input, node_grad_pre) * node_scale,
            ("dom", "sub"),
            scatter_dimension=0,
            tiled=True,
        ),
        lax.psum_scatter(
            inner(node_act, node_grad_z) * node_scale,
            ("dom", "sub"),
            scatter_dimension=0,
            tiled=True,
        ),
    )
    node_grad_input = outer_back(node_grad_pre, full_node_first)
    state_grads = node_upstream + node_grad_input[:, :width]
    edge_upstream = (
        edge_cotangent + jnp.take(node_grad_input[:, width:], target, axis=0)
    ) * live_edges
    edge_grad_z = norm_back(edge_upstream * full_edge_gain, edge_normed, edge_inverse)
    edge_grad_pre = outer_back(edge_grad_z, full_edge_second) * (edge_pre > 0).astype(jnp.float32)
    edge_second_grad = lax.psum_scatter(
        inner(edge_act, edge_grad_z) * edge_scale, ("dom", "sub"), scatter_dimension=0, tiled=True
    )
    extended = jnp.concatenate([node_states, ghosts], axis=0)
    features = jnp.concatenate(
        [edge_states, jnp.take(extended, source, axis=0), jnp.take(extended, target, axis=0)],
        axis=1,
    )
    edge_first_grad = lax.psum_scatter(
        inner(features, edge_grad_pre) * edge_scale, ("dom", "sub"), scatter_dimension=0, tiled=True
    )
    edge_grad_input = outer_back(edge_grad_pre, full_edge_first)
    edge_grads = (edge_cotangent + edge_grad_input[:, :width]) * live_edges
    extended_grads = jax.ops.segment_sum(
        edge_grad_input[:, width : 2 * width], source, node_rows + 4 * ghost
    )
    extended_grads = extended_grads + jax.ops.segment_sum(
        edge_grad_input[:, 2 * width :], target, node_rows + 4 * ghost
    )
    state_grads = state_grads + extended_grads[:node_rows]
    ghost_grads = extended_grads[node_rows:].reshape(4, ghost, width)
    dom_back = padded(jnp.stack([ghost_grads[0], ghost_grads[1]]), (("dom", 0),), 1)
    sub_back = padded(jnp.stack([ghost_grads[2], ghost_grads[3]]), (("sub", 0),), 1)
    returned = jnp.stack([dom_back[3], dom_back[0], sub_back[3], sub_back[0]])
    state_grads = state_grads + jax.ops.segment_sum(
        returned.reshape(-1, width), lists.reshape(-1), node_rows
    )
    return (
        edge_grads,
        state_grads,
        edge_first_grad,
        edge_second_grad,
        node_first_grad,
        node_second_grad,
    )


MESH = pl.DeviceIdType.MESH
UNIT = 32


def split(values):
    high = values.astype(jnp.bfloat16)
    return (high, (values - high.astype(jnp.float32)).astype(jnp.bfloat16))


def product(left, right, dims):
    return lax.dot_general(
        left, right, ((dims[:1], dims[1:]), ((), ())), preferred_element_type=jnp.float32
    )


def wide(left, right, dims):
    return (
        product(left[0], right[1], dims)
        + product(left[1], right[0], dims)
        + product(left[0], right[0], dims)
    )


def picked(picks, right, dims=(1, 0)):
    return product(picks, right[1], dims) + product(picks, right[0], dims)


def picks_of(slots, rows, first=0):
    place = lax.broadcasted_iota(jnp.int32, (rows, slots.shape[1]), 0) + first
    ones = jnp.where(place == slots, 1.0, 0.0).astype(jnp.float32)
    return (ones.astype(jnp.bfloat16), ones.T.astype(jnp.bfloat16))


def layer_kernel(
    edge_scale,
    node_scale,
    counts,
    blocks,
    endpoints,
    lists,
    node_states,
    node_pre,
    edge_states,
    edge_pre,
    node_cotangent,
    edge_cotangent,
    own_a,
    own_b,
    own_c,
    own_d,
    edge_grads,
    node_grads,
    edge_first_grad,
    edge_second_grad,
    node_first_grad,
    node_second_grad,
    all_a,
    all_b,
    all_c,
    all_d,
    sum_b,
    sum_c,
    sum_a,
    sum_d,
    from_core,
    from_x,
    from_sub,
    outgoing,
    ghosts,
    ghost_grads,
    returned,
    gather_send,
    gather_recv,
    core_send,
    core_recv,
    x_send,
    x_recv,
    sub_send,
    sub_recv,
    halo_send,
    halo_recv,
):
    doms = all_a.shape[0]
    subs = all_a.shape[1]
    width = node_states.shape[1]
    node_rows = node_states.shape[0]
    edge_rows = edge_states.shape[0]
    ghost = outgoing.shape[1]
    dom = lax.axis_index("dom")
    sub = lax.axis_index("sub")
    group = lax.axis_index("groups")
    x_mate = lax.rem(dom + 2, doms)
    core_mate = dom + 1 - 2 * lax.rem(dom, 2)
    far_mate = x_mate + 1 - 2 * lax.rem(x_mate, 2)

    def before(step):
        return lax.rem(sub + subs - step, subs)

    def after(step):
        return lax.rem(sub + step, subs)

    barrier = pltpu.get_barrier_semaphore()
    for step in range(1, doms):
        pl.semaphore_signal(
            barrier, inc=1, device_id={"dom": lax.rem(dom + step, doms)}, device_id_type=MESH
        )
    for step in range(1, subs):
        pl.semaphore_signal(barrier, inc=1, device_id={"sub": after(step)}, device_id_type=MESH)
    pl.semaphore_signal(barrier, inc=1, device_id={"groups": 1 - group}, device_id_type=MESH)
    pl.semaphore_wait(barrier, doms + subs - 1)

    def remote(source, target, send, recv, device):
        return pltpu.make_async_remote_copy(
            src_ref=source,
            dst_ref=target,
            send_sem=send,
            recv_sem=recv,
            device_id=device,
            device_id_type=MESH,
        )

    owns = (own_a, own_b, own_c, own_d)
    alls = (all_a, all_b, all_c, all_d)
    shared = (False, False, True, True)
    pending = []

    def rows_of(ref, part, half):
        if half is None or not shared[part]:
            return ref
        count = owns[part].shape[0] // 2
        return ref.at[pl.ds(pl.multiple_of(half * count, 16), count), :]

    def place_of(part, slot, half):
        return rows_of(alls[part].at[slot[0], slot[1]], part, half)

    def gather_copy(part, index, source, target, device):
        return remote(
            source, target, gather_send.at[part, index], gather_recv.at[part, index], device
        )

    def gather_start(part, index, slot, half, device, own=False):
        target = place_of(part, slot, half)
        source = rows_of(owns[part], part, half) if own else target
        copy = gather_copy(part, index, source, target, device)
        copy.start()
        pending.append(copy)

    def gather_wait(part, index, slot, half):
        place = place_of(part, slot, half)
        gather_copy(part, index, place, place, {"dom": core_mate}).wait_recv()

    SUB, X = 0, subs - 1
    CORE_NEAR, CORE_FAR = 2 * subs - 1, 3 * subs - 1
    Y_NEAR, Y_FAR = 4 * subs - 1, 5 * subs - 1
    LATE_NEAR, LATE_FAR = 6 * subs - 1, 7 * subs - 1
    to_x, to_core, to_y = {"dom": x_mate}, {"dom": core_mate}, {"groups": 1 - group}

    def gather_first(part):
        for step in range(1, subs):
            gather_start(part, SUB + step - 1, (dom, sub), group, {"sub": after(step)}, True)
        gather_start(part, X, (dom, sub), group, to_x, True)
        gather_start(part, CORE_NEAR, (dom, sub), None, to_core, True)

    def gather_from_sub(part, steps=range(1, subs)):
        for step in steps:
            slot = (dom, before(step))
            gather_wait(part, SUB + step - 1, slot, group)
            gather_start(part, X + step, slot, group, to_x)
            if shared[part]:
                gather_start(part, Y_NEAR + step, slot, group, to_y)
            gather_start(part, CORE_NEAR + step, slot, group, to_core)

    def gather_from_x(part):
        for step in range(subs):
            slot = (x_mate, before(step))
            gather_wait(part, X + step, slot, group)
            if shared[part]:
                gather_start(part, Y_FAR + step, slot, group, to_y)
            gather_start(part, CORE_FAR + step, slot, group, to_core)

    def gather_from_y(part):
        for step in range(1, subs):
            slot = (dom, before(step))
            gather_wait(part, Y_NEAR + step, slot, 1 - group)
            gather_start(part, LATE_NEAR + step, slot, 1 - group, to_core)
        for step in range(subs):
            slot = (x_mate, before(step))
            gather_wait(part, Y_FAR + step, slot, 1 - group)
            gather_start(part, LATE_FAR + step, slot, 1 - group, to_core)

    def gather_from_core(part):
        for step in range(subs):
            near, far = (core_mate, before(step)), (far_mate, before(step))
            gather_wait(part, CORE_NEAR + step, near, group if step else None)
            gather_wait(part, CORE_FAR + step, far, group)
            if shared[part]:
                if step:
                    gather_wait(part, LATE_NEAR + step, near, 1 - group)
                gather_wait(part, LATE_FAR + step, far, 1 - group)

    sums = (sum_b, sum_c, sum_a, sum_d)
    results = (node_second_grad, node_first_grad, edge_second_grad, edge_first_grad)
    units = [
        (which, first)
        for which in range(4)
        for first in range(0, sums[which].shape[2], UNIT)
    ]

    def unit_rows(unit, which_dom):
        which, first = units[unit]
        return sums[which].at[which_dom, :, pl.ds(first, UNIT), :]

    def core_copies(unit):
        return [
            remote(
                unit_rows(unit, target),
                from_core.at[unit, index],
                core_send.at[unit, index],
                core_recv.at[unit, index],
                {"dom": core_mate},
            )
            for index, target in enumerate((far_mate, core_mate))
        ]

    def x_copy(unit):
        return remote(
            unit_rows(unit, x_mate),
            from_x.at[unit],
            x_send.at[unit],
            x_recv.at[unit],
            {"dom": x_mate},
        )

    def sub_copies(unit):
        which, first = units[unit]
        return [
            remote(
                sums[which].at[dom, after(step), pl.ds(first, UNIT), :],
                from_sub.at[unit, step - 1],
                sub_send.at[unit, step - 1],
                sub_recv.at[unit, step - 1],
                {"sub": after(step)},
            )
            for step in range(1, subs)
        ]

    def reduce_core(unit):
        for copy in core_copies(unit):
            copy.start()

    def reduce_x(unit):
        far, near = core_copies(unit)
        far.wait_recv()
        rows = unit_rows(unit, x_mate)
        rows[...] = rows[...] + from_core[unit, 0]
        x_copy(unit).start()
        near.wait_recv()
        rows = unit_rows(unit, dom)
        rows[...] = rows[...] + from_core[unit, 1]

    def reduce_sub(unit):
        x_copy(unit).wait_recv()
        rows = unit_rows(unit, dom)
        rows[...] = rows[...] + from_x[unit]
        for copy in sub_copies(unit):
            copy.start()

    def reduce_last(unit):
        which, first = units[unit]
        total = sums[which][dom, sub, pl.ds(first, UNIT), :]
        for step, copy in enumerate(sub_copies(unit)):
            copy.wait_recv()
            total = total + from_sub[unit, step]
        results[which][pl.ds(first, UNIT), :] = total

    def halo_copies(source, target, turn):
        ways = (
            {"dom": lax.rem(dom + 1, doms)},
            {"dom": lax.rem(dom + doms - 1, doms)},
            {"sub": after(1)},
            {"sub": before(1)},
        )
        return [
            remote(
                source.at[index],
                target.at[index],
                halo_send.at[turn, index],
                halo_recv.at[turn, index],
                ways[index + (1 - 2 * (index % 2)) * turn],
            )
            for index in range(4)
        ]

    for part in range(2):
        gather_first(part)
    for part in range(4):
        alls[part][dom, sub] = owns[part][...]

    states = split(node_states[...])
    list_picks, list_back = picks_of(lists[...], node_rows)
    outgoing[...] = picked(list_back, states).reshape(4, ghost, width)
    ghost_copies = halo_copies(outgoing, ghosts, 0)
    for copy in ghost_copies:
        copy.start()
    target_picks, target_back = picks_of(endpoints[1:2, :], node_rows)
    source_picks, source_back = picks_of(endpoints[0:1, :], node_rows)
    ghost_picks, ghost_back = picks_of(endpoints[0:1, :], 4 * ghost, node_rows)
    live_nodes = jnp.where(
        lax.broadcasted_iota(jnp.int32, (node_rows, 1), 0) < counts[0], 1.0, 0.0
    ).astype(jnp.float32)
    live_edges = jnp.where(
        lax.broadcasted_iota(jnp.int32, (edge_rows, 1), 0) < blocks[0] * 128, 1.0, 0.0
    ).astype(jnp.float32)
    edge_act = split(jnp.maximum(edge_pre[...], 0.0))
    node_act = split(jnp.maximum(node_pre[...], 0.0))

    gather_from_sub(0)
    gather_first(2)
    gather_from_sub(1)
    gather_first(3)
    gather_from_x(0)
    gather_from_core(0)
    second_rows = width // (doms * subs)
    node_second = split(all_a[:, :, :second_rows, :].reshape(width, width))
    params = jnp.sum(
        all_a[:, :, second_rows:, :].reshape(doms * subs, -1, width), axis=0
    )
    edge_bias, edge_gain, edge_shift, node_bias, node_gain = (
        params[row : row + 1, :] for row in range(5)
    )
    node_normed, node_inverse = layer_norm(wide(node_act, node_second, (1, 0)) + node_bias)
    gather_from_x(1)
    gather_from_sub(2, [1])
    node_upstream = node_cotangent[...] * live_nodes
    node_grad_z = split(norm_back(node_upstream * node_gain, node_normed, node_inverse))
    gather_from_sub(2, range(2, subs))
    sum_b[...] = (wide(node_act, node_grad_z, (0, 0)) * node_scale).reshape(sum_b.shape)
    reduce_core(0)
    gather_from_core(1)
    edge_second = split(all_b[...].reshape(width, width))
    edge_normed, edge_inverse = layer_norm(wide(edge_act, edge_second, (1, 0)) + edge_bias)
    message = (edge_normed * edge_gain + edge_shift) * live_edges
    aggregate = split(picked(target_picks, split(message)))
    gather_from_x(2)
    gather_from_sub(3, [1])
    reduce_x(0)
    node_grad_pre = split(
        wide(node_grad_z, node_second, (1, 1)) * (node_pre[...] > 0).astype(jnp.float32)
    )
    gather_from_sub(3, range(2, subs))
    sum_c[: doms // 2] = (wide(states, node_grad_pre, (0, 0)) * node_scale).reshape(
        doms // 2, *sum_c.shape[1:]
    )
    gather_from_y(2)
    sum_c[doms // 2 :] = (wide(aggregate, node_grad_pre, (0, 0)) * node_scale).reshape(
        doms // 2, *sum_c.shape[1:]
    )
    reduce_core(1)
    reduce_core(2)
    gather_from_x(3)
    gather_from_core(2)
    reduce_x(1)
    reduce_x(2)

    node_first = split(all_c[...].reshape(2 * width, width))
    from_nodes = wide(
        node_grad_pre, tuple(half[width:] for half in node_first), (1, 1)
    )
    edge_upstream = (edge_cotangent[...] + picked(target_back, split(from_nodes))) * live_edges
    edge_grad_z = split(norm_back(edge_upstream * edge_gain, edge_normed, edge_inverse))
    sum_a[...] = (wide(edge_act, edge_grad_z, (0, 0)) * edge_scale).reshape(sum_a.shape)
    reduce_core(3)
    reduce_sub(0)
    gather_from_y(3)
    edge_grad_pre = split(
        wide(edge_grad_z, edge_second, (1, 1)) * (edge_pre[...] > 0).astype(jnp.float32)
    )
    for copy in ghost_copies:
        copy.wait_recv()
    sender = picked(source_back, states) + picked(
        ghost_back, split(ghosts[...].reshape(4 * ghost, width))
    )
    receiver = picked(target_back, states)
    reduce_x(3)
    first_grad = jnp.concatenate(
        [
            wide(split(feature), edge_grad_pre, (0, 0)) * edge_scale
            for feature in (edge_states[...], sender, receiver)
        ],
        axis=0,
    )
    sum_d[...] = first_grad.reshape(sum_d.shape)
    for unit in range(4, len(units)):
        reduce_core(unit)
    reduce_sub(1)
    for unit in range(4, len(units)):
        reduce_x(unit)
    reduce_sub(2)
    state_grads = node_upstream + wide(
        node_grad_pre, tuple(half[:width] for half in node_first), (1, 1)
    )

    gather_from_core(3)
    edge_first = split(all_d[...].reshape(3 * width, width))

    def edge_part(index):
        rows = slice(index * width, (index + 1) * width)
        return wide(edge_grad_pre, tuple(half[rows] for half in edge_first), (1, 1))

    sender_grads = split(edge_part(1))
    ghost_grads[...] = picked(ghost_picks, sender_grads).reshape(4, ghost, width)
    return_copies = halo_copies(ghost_grads, returned, 1)
    for copy in return_copies:
        copy.start()
    for unit in range(3, 5):
        reduce_sub(unit)
    edge_grads[...] = (edge_cotangent[...] + edge_part(0)) * live_edges
    state_grads = state_grads + picked(source_picks, sender_grads)
    state_grads = state_grads + picked(target_picks, split(edge_part(2)))
    for unit in range(5, len(units)):
        reduce_sub(unit)
    for copy in return_copies:
        copy.wait_recv()
    node_grads[...] = state_grads + picked(
        list_picks, split(returned[...].reshape(4 * ghost, width))
    )
    for unit in range(len(units)):
        reduce_last(unit)

    for copy in pending + ghost_copies + return_copies:
        copy.wait_send()
    for unit in range(len(units)):
        for copy in core_copies(unit) + [x_copy(unit)] + sub_copies(unit):
            copy.wait_send()


def kernel_shards(
    node_states,
    node_pre,
    edge_states,
    edge_pre,
    node_cotangent,
    edge_cotangent,
    endpoints,
    send_lists,
    node_counts,
    edge_blocks,
    edge_first,
    edge_second,
    edge_bias,
    edge_gain,
    edge_shift,
    node_first,
    node_second,
    node_bias,
    node_gain,
):
    node_rows, width = node_states.shape
    edge_rows = edge_states.shape[0]
    ghost = send_lists.shape[2]
    doms, subs = lax.axis_size("dom"), lax.axis_size("sub")
    peers = doms * subs
    mine = lax.axis_index("dom") * subs + lax.axis_index("sub")
    place = jnp.arange(width) // (width // peers) == mine
    vectors = jnp.stack([edge_bias, edge_gain, edge_shift, node_bias, node_gain])
    spread = jnp.where(place[None, :], jnp.tile(vectors, (1, peers)), 0.0)
    own_a = jnp.concatenate([node_second, spread, jnp.zeros((3, width), jnp.float32)], axis=0)
    owns = (own_a, edge_second, node_first, edge_first)
    sums = (node_second, node_first, edge_second, edge_first)
    units = sum(shard.shape[0] for shard in sums) // UNIT
    vmem = pl.BlockSpec(memory_space=pltpu.VMEM)
    smem = pl.BlockSpec(memory_space=pltpu.SMEM)
    f32 = jnp.float32
    dma = pltpu.SemaphoreType.DMA
    halo = pltpu.VMEM((4, ghost, width), f32)
    return pl.pallas_call(
        functools.partial(
            layer_kernel,
            1.0 / math.sqrt(edge_rows * peers),
            1.0 / math.sqrt(node_rows * peers),
        ),
        out_shape=[
            jax.ShapeDtypeStruct(shape, f32)
            for shape in (
                edge_states.shape,
                node_states.shape,
                edge_first.shape,
                edge_second.shape,
                node_first.shape,
                node_second.shape,
            )
        ],
        in_specs=[smem, smem] + [vmem] * 12,
        out_specs=[vmem] * 6,
        scratch_shapes=[pltpu.VMEM((doms, subs) + own.shape, f32) for own in owns]
        + [pltpu.VMEM((doms, subs) + shard.shape, f32) for shard in sums]
        + [
            pltpu.VMEM((units, 2, subs, UNIT, width), f32),
            pltpu.VMEM((units, subs, UNIT, width), f32),
            pltpu.VMEM((units, subs - 1, UNIT, width), f32),
            halo,
            halo,
            halo,
            halo,
            dma((4, 8 * subs - 1)),
            dma((4, 8 * subs - 1)),
            dma((units, 2)),
            dma((units, 2)),
            dma((units,)),
            dma((units,)),
            dma((units, subs - 1)),
            dma((units, subs - 1)),
            dma((2, 4)),
            dma((2, 4)),
        ],
        compiler_params=pltpu.CompilerParams(
            collective_id=0, has_side_effects=True, vmem_limit_bytes=56 * 2**20
        ),
    )(
        node_counts,
        edge_blocks,
        endpoints,
        send_lists.reshape(1, 4 * ghost),
        node_states,
        node_pre,
        edge_states,
        edge_pre,
        node_cotangent,
        edge_cotangent,
        *owns,
    )


def shards(*blocks):
    weights = (blocks[10], blocks[11], blocks[15], blocks[16])
    fits = all(weight.shape[0] % UNIT == 0 for weight in weights)
    paired = lax.axis_size("groups") == 2 and lax.axis_size("dom") == 4
    if paired and lax.axis_size("sub") > 2 and fits:
        return tuple(kernel_shards(*blocks))
    return plain_shards(*blocks)


def solution(mesh):
    in_specs = (
        P(("groups", "dom", "sub"), None),
        P(("groups", "dom", "sub"), None),
        P(("groups", "dom", "sub"), None),
        P(("groups", "dom", "sub"), None),
        P(("groups", "dom", "sub"), None),
        P(("groups", "dom", "sub"), None),
        P(None, ("groups", "dom", "sub")),
        P(("groups", "dom", "sub"), None, None),
        P(("groups", "dom", "sub")),
        P(("groups", "dom", "sub")),
        P(("dom", "sub"), None),
        P(("dom", "sub"), None),
        P(("dom", "sub")),
        P(("dom", "sub")),
        P(("dom", "sub")),
        P(("dom", "sub"), None),
        P(("dom", "sub"), None),
        P(("dom", "sub")),
        P(("dom", "sub")),
    )
    out_specs = (
        P(("groups", "dom", "sub"), None),
        P(("groups", "dom", "sub"), None),
        P(("groups", "dom", "sub"), None),
        P(("groups", "dom", "sub"), None),
        P(("groups", "dom", "sub"), None),
        P(("groups", "dom", "sub"), None),
    )
    return jax.shard_map(shards, mesh=mesh, in_specs=in_specs, out_specs=out_specs, check_vma=False)
```

```python
import functools
import math

import jax
import jax.numpy as jnp
from jax import lax
from jax.experimental import pallas as pl
from jax.experimental.pallas import tpu as pltpu
from jax.sharding import PartitionSpec as P

EPSILON = 1e-05


def padded(cells, sides, width):
    for axis, dim in sides:
        count = lax.axis_size(axis)
        ends = count - 1
        head = lax.slice_in_dim(cells, 0, width, axis=dim)
        tail = lax.slice_in_dim(cells, cells.shape[dim] - width, cells.shape[dim], axis=dim)
        cells = jnp.concatenate(
            [
                lax.ppermute(tail, axis, [(i, (i + 1) % count) for i in range(ends)]),
                cells,
                lax.ppermute(head, axis, [((i + 1) % count, i) for i in range(ends)]),
            ],
            axis=dim,
        )
    return cells


def matmul(left, right):
    return jnp.dot(left, right, precision=lax.Precision.HIGHEST, preferred_element_type=jnp.float32)


def inner(left, right):
    return lax.dot_general(
        left,
        right,
        (((0,), (0,)), ((), ())),
        precision=lax.Precision.HIGHEST,
        preferred_element_type=jnp.float32,
    )


def outer_back(left, right):
    return lax.dot_general(
        left,
        right,
        (((1,), (1,)), ((), ())),
        precision=lax.Precision.HIGHEST,
        preferred_element_type=jnp.float32,
    )


def layer_norm(values):
    center = values - jnp.mean(values, axis=-1, keepdims=True)
    inverse = 1.0 / jnp.sqrt(jnp.mean(center * center, axis=-1, keepdims=True) + EPSILON)
    return (center * inverse, inverse)


def norm_back(upstream, normed, inverse):
    first = jnp.mean(upstream, axis=-1, keepdims=True)
    second = jnp.mean(upstream * normed, axis=-1, keepdims=True)
    return inverse * (upstream - first - normed * second)


def plain_shards(
    node_states,
    node_pre,
    edge_states,
    edge_pre,
    node_cotangent,
    edge_cotangent,
    endpoints,
    send_lists,
    node_counts,
    edge_blocks,
    edge_first,
    edge_second,
    edge_bias,
    edge_gain,
    edge_shift,
    node_first,
    node_second,
    node_bias,
    node_gain,
):
    node_rows, width = node_states.shape
    edge_rows = edge_states.shape[0]
    ghost = send_lists.shape[2]
    dom_count = lax.axis_size("dom")
    sub_count = lax.axis_size("sub")
    peer_count = dom_count * sub_count
    lists = send_lists[0]
    outgoing = jnp.take(node_states, lists.reshape(-1), axis=0).reshape(4, ghost, width)
    dom_side = padded(jnp.stack([outgoing[1], outgoing[0]]), (("dom", 0),), 1)
    sub_side = padded(jnp.stack([outgoing[3], outgoing[2]]), (("sub", 0),), 1)
    ghosts = jnp.stack([dom_side[0], dom_side[3], sub_side[0], sub_side[3]])
    ghosts = ghosts.reshape(4 * ghost, width)
    full_node_first, full_node_second, full_node_bias, full_node_gain = (
        lax.all_gather(node_first, ("dom", "sub"), axis=0, tiled=True),
        lax.all_gather(node_second, ("dom", "sub"), axis=0, tiled=True),
        lax.all_gather(node_bias, ("dom", "sub"), axis=0, tiled=True),
        lax.all_gather(node_gain, ("dom", "sub"), axis=0, tiled=True),
    )
    full_edge_first, full_edge_second, full_edge_bias, full_edge_gain, full_edge_shift = (
        lax.all_gather(edge_first, ("dom", "sub"), axis=0, tiled=True),
        lax.all_gather(edge_second, ("dom", "sub"), axis=0, tiled=True),
        lax.all_gather(edge_bias, ("dom", "sub"), axis=0, tiled=True),
        lax.all_gather(edge_gain, ("dom", "sub"), axis=0, tiled=True),
        lax.all_gather(edge_shift, ("dom", "sub"), axis=0, tiled=True),
    )
    live_nodes = (jnp.arange(node_rows) < node_counts[0]).astype(jnp.float32)[:, None]
    live_edges = (jnp.arange(edge_rows) < edge_blocks[0] * 128).astype(jnp.float32)[:, None]
    source = endpoints[0]
    target = endpoints[1]
    edge_scale = 1.0 / math.sqrt(edge_rows * peer_count)
    node_scale = 1.0 / math.sqrt(node_rows * peer_count)
    edge_act = jnp.maximum(edge_pre, 0.0)
    edge_normed, edge_inverse = layer_norm(matmul(edge_act, full_edge_second) + full_edge_bias)
    message = (edge_normed * full_edge_gain + full_edge_shift) * live_edges
    aggregate = jax.ops.segment_sum(message, target, node_rows)
    node_act = jnp.maximum(node_pre, 0.0)
    node_normed, node_inverse = layer_norm(matmul(node_act, full_node_second) + full_node_bias)
    node_upstream = node_cotangent * live_nodes
    node_grad_z = norm_back(node_upstream * full_node_gain, node_normed, node_inverse)
    node_grad_pre = outer_back(node_grad_z, full_node_second) * (node_pre > 0).astype(jnp.float32)
    node_input = jnp.concatenate([node_states, aggregate], axis=1)
    node_first_grad, node_second_grad = (
        lax.psum_scatter(
            inner(node_input, node_grad_pre) * node_scale,
            ("dom", "sub"),
            scatter_dimension=0,
            tiled=True,
        ),
        lax.psum_scatter(
            inner(node_act, node_grad_z) * node_scale,
            ("dom", "sub"),
            scatter_dimension=0,
            tiled=True,
        ),
    )
    node_grad_input = outer_back(node_grad_pre, full_node_first)
    state_grads = node_upstream + node_grad_input[:, :width]
    edge_upstream = (
        edge_cotangent + jnp.take(node_grad_input[:, width:], target, axis=0)
    ) * live_edges
    edge_grad_z = norm_back(edge_upstream * full_edge_gain, edge_normed, edge_inverse)
    edge_grad_pre = outer_back(edge_grad_z, full_edge_second) * (edge_pre > 0).astype(jnp.float32)
    edge_second_grad = lax.psum_scatter(
        inner(edge_act, edge_grad_z) * edge_scale, ("dom", "sub"), scatter_dimension=0, tiled=True
    )
    extended = jnp.concatenate([node_states, ghosts], axis=0)
    features = jnp.concatenate(
        [edge_states, jnp.take(extended, source, axis=0), jnp.take(extended, target, axis=0)],
        axis=1,
    )
    edge_first_grad = lax.psum_scatter(
        inner(features, edge_grad_pre) * edge_scale, ("dom", "sub"), scatter_dimension=0, tiled=True
    )
    edge_grad_input = outer_back(edge_grad_pre, full_edge_first)
    edge_grads = (edge_cotangent + edge_grad_input[:, :width]) * live_edges
    extended_grads = jax.ops.segment_sum(
        edge_grad_input[:, width : 2 * width], source, node_rows + 4 * ghost
    )
    extended_grads = extended_grads + jax.ops.segment_sum(
        edge_grad_input[:, 2 * width :], target, node_rows + 4 * ghost
    )
    state_grads = state_grads + extended_grads[:node_rows]
    ghost_grads = extended_grads[node_rows:].reshape(4, ghost, width)
    dom_back = padded(jnp.stack([ghost_grads[0], ghost_grads[1]]), (("dom", 0),), 1)
    sub_back = padded(jnp.stack([ghost_grads[2], ghost_grads[3]]), (("sub", 0),), 1)
    returned = jnp.stack([dom_back[3], dom_back[0], sub_back[3], sub_back[0]])
    state_grads = state_grads + jax.ops.segment_sum(
        returned.reshape(-1, width), lists.reshape(-1), node_rows
    )
    return (
        edge_grads,
        state_grads,
        edge_first_grad,
        edge_second_grad,
        node_first_grad,
        node_second_grad,
    )


MESH = pl.DeviceIdType.MESH
UNIT = 32


def split(values):
    high = values.astype(jnp.bfloat16)
    return (high, (values - high.astype(jnp.float32)).astype(jnp.bfloat16))


def product(left, right, dims):
    return lax.dot_general(
        left, right, ((dims[:1], dims[1:]), ((), ())), preferred_element_type=jnp.float32
    )


def wide(left, right, dims):
    return (
        product(left[0], right[1], dims)
        + product(left[1], right[0], dims)
        + product(left[0], right[0], dims)
    )


def picked(picks, right, dims=(1, 0)):
    return product(picks, right[1], dims) + product(picks, right[0], dims)


def picks_of(slots, rows, first=0):
    place = lax.broadcasted_iota(jnp.int32, (rows, slots.shape[1]), 0) + first
    ones = jnp.where(place == slots, 1.0, 0.0).astype(jnp.float32)
    return (ones.astype(jnp.bfloat16), ones.T.astype(jnp.bfloat16))


def layer_kernel(
    edge_scale,
    node_scale,
    counts,
    blocks,
    endpoints,
    lists,
    node_states,
    node_pre,
    edge_states,
    edge_pre,
    node_cotangent,
    edge_cotangent,
    own_a,
    own_b,
    own_c,
    own_d,
    edge_grads,
    node_grads,
    edge_first_grad,
    edge_second_grad,
    node_first_grad,
    node_second_grad,
    all_a,
    all_b,
    all_c,
    all_d,
    sum_b,
    sum_c,
    sum_a,
    sum_d,
    from_core,
    from_x,
    from_sub,
    outgoing,
    ghosts,
    ghost_grads,
    returned,
    gather_send,
    gather_recv,
    core_send,
    core_recv,
    x_send,
    x_recv,
    sub_send,
    sub_recv,
    halo_send,
    halo_recv,
):
    doms = all_a.shape[0]
    subs = all_a.shape[1]
    width = node_states.shape[1]
    node_rows = node_states.shape[0]
    edge_rows = edge_states.shape[0]
    ghost = outgoing.shape[1]
    dom = lax.axis_index("dom")
    sub = lax.axis_index("sub")
    group = lax.axis_index("groups")
    x_mate = lax.rem(dom + 2, doms)
    core_mate = dom + 1 - 2 * lax.rem(dom, 2)
    far_mate = x_mate + 1 - 2 * lax.rem(x_mate, 2)

    def before(step):
        return lax.rem(sub + subs - step, subs)

    def after(step):
        return lax.rem(sub + step, subs)

    barrier = pltpu.get_barrier_semaphore()
    for step in range(1, doms):
        pl.semaphore_signal(
            barrier, inc=1, device_id={"dom": lax.rem(dom + step, doms)}, device_id_type=MESH
        )
    for step in range(1, subs):
        pl.semaphore_signal(barrier, inc=1, device_id={"sub": after(step)}, device_id_type=MESH)
    pl.semaphore_signal(barrier, inc=1, device_id={"groups": 1 - group}, device_id_type=MESH)
    pl.semaphore_wait(barrier, doms + subs - 1)

    def remote(source, target, send, recv, device):
        return pltpu.make_async_remote_copy(
            src_ref=source,
            dst_ref=target,
            send_sem=send,
            recv_sem=recv,
            device_id=device,
            device_id_type=MESH,
        )

    owns = (own_a, own_b, own_c, own_d)
    alls = (all_a, all_b, all_c, all_d)
    shared = (False, False, True, True)
    pending = []

    def rows_of(ref, part, half):
        if half is None or not shared[part]:
            return ref
        count = owns[part].shape[0] // 2
        return ref.at[pl.ds(pl.multiple_of(half * count, 16), count), :]

    def place_of(part, slot, half):
        return rows_of(alls[part].at[slot[0], slot[1]], part, half)

    def gather_copy(part, index, source, target, device):
        return remote(
            source, target, gather_send.at[part, index], gather_recv.at[part, index], device
        )

    def gather_start(part, index, slot, half, device, own=False):
        target = place_of(part, slot, half)
        source = rows_of(owns[part], part, half) if own else target
        copy = gather_copy(part, index, source, target, device)
        copy.start()
        pending.append(copy)

    def gather_wait(part, index, slot, half):
        place = place_of(part, slot, half)
        gather_copy(part, index, place, place, {"dom": core_mate}).wait_recv()

    SUB, X = 0, subs - 1
    CORE_NEAR, CORE_FAR = 2 * subs - 1, 3 * subs - 1
    Y_NEAR, Y_FAR = 4 * subs - 1, 5 * subs - 1
    LATE_NEAR, LATE_FAR = 6 * subs - 1, 7 * subs - 1
    to_x, to_core, to_y = {"dom": x_mate}, {"dom": core_mate}, {"groups": 1 - group}

    def gather_first(part):
        for step in range(1, subs):
            gather_start(part, SUB + step - 1, (dom, sub), group, {"sub": after(step)}, True)
        gather_start(part, X, (dom, sub), group, to_x, True)
        gather_start(part, CORE_NEAR, (dom, sub), None, to_core, True)

    def gather_from_sub(part, steps=range(1, subs)):
        for step in steps:
            slot = (dom, before(step))
            gather_wait(part, SUB + step - 1, slot, group)
            gather_start(part, X + step, slot, group, to_x)
            if shared[part]:
                gather_start(part, Y_NEAR + step, slot, group, to_y)
            gather_start(part, CORE_NEAR + step, slot, group, to_core)

    def gather_from_x(part):
        for step in range(subs):
            slot = (x_mate, before(step))
            gather_wait(part, X + step, slot, group)
            if shared[part]:
                gather_start(part, Y_FAR + step, slot, group, to_y)
            gather_start(part, CORE_FAR + step, slot, group, to_core)

    def gather_from_y(part):
        for step in range(1, subs):
            slot = (dom, before(step))
            gather_wait(part, Y_NEAR + step, slot, 1 - group)
            gather_start(part, LATE_NEAR + step, slot, 1 - group, to_core)
        for step in range(subs):
            slot = (x_mate, before(step))
            gather_wait(part, Y_FAR + step, slot, 1 - group)
            gather_start(part, LATE_FAR + step, slot, 1 - group, to_core)

    def gather_from_core(part):
        for step in range(subs):
            near, far = (core_mate, before(step)), (far_mate, before(step))
            gather_wait(part, CORE_NEAR + step, near, group if step else None)
            gather_wait(part, CORE_FAR + step, far, group)
            if shared[part]:
                if step:
                    gather_wait(part, LATE_NEAR + step, near, 1 - group)
                gather_wait(part, LATE_FAR + step, far, 1 - group)

    sums = (sum_b, sum_c, sum_a, sum_d)
    results = (node_second_grad, node_first_grad, edge_second_grad, edge_first_grad)
    units = [
        (which, first)
        for which in range(4)
        for first in range(0, sums[which].shape[2], UNIT)
    ]

    def unit_rows(unit, which_dom):
        which, first = units[unit]
        return sums[which].at[which_dom, :, pl.ds(first, UNIT), :]

    def core_copies(unit):
        return [
            remote(
                unit_rows(unit, target),
                from_core.at[unit, index],
                core_send.at[unit, index],
                core_recv.at[unit, index],
                {"dom": core_mate},
            )
            for index, target in enumerate((far_mate, core_mate))
        ]

    def x_copy(unit):
        return remote(
            unit_rows(unit, x_mate),
            from_x.at[unit],
            x_send.at[unit],
            x_recv.at[unit],
            {"dom": x_mate},
        )

    def sub_copies(unit):
        which, first = units[unit]
        return [
            remote(
                sums[which].at[dom, after(step), pl.ds(first, UNIT), :],
                from_sub.at[unit, step - 1],
                sub_send.at[unit, step - 1],
                sub_recv.at[unit, step - 1],
                {"sub": after(step)},
            )
            for step in range(1, subs)
        ]

    def reduce_core(unit):
        for copy in core_copies(unit):
            copy.start()

    def reduce_x(unit):
        far, near = core_copies(unit)
        far.wait_recv()
        rows = unit_rows(unit, x_mate)
        rows[...] = rows[...] + from_core[unit, 0]
        x_copy(unit).start()
        near.wait_recv()
        rows = unit_rows(unit, dom)
        rows[...] = rows[...] + from_core[unit, 1]

    def reduce_sub(unit):
        x_copy(unit).wait_recv()
        rows = unit_rows(unit, dom)
        rows[...] = rows[...] + from_x[unit]
        for copy in sub_copies(unit):
            copy.start()

    def reduce_last(unit):
        which, first = units[unit]
        total = sums[which][dom, sub, pl.ds(first, UNIT), :]
        for step, copy in enumerate(sub_copies(unit)):
            copy.wait_recv()
            total = total + from_sub[unit, step]
        results[which][pl.ds(first, UNIT), :] = total

    def halo_copies(source, target, turn):
        ways = (
            {"dom": lax.rem(dom + 1, doms)},
            {"dom": lax.rem(dom + doms - 1, doms)},
            {"sub": after(1)},
            {"sub": before(1)},
        )
        return [
            remote(
                source.at[index],
                target.at[index],
                halo_send.at[turn, index],
                halo_recv.at[turn, index],
                ways[index + (1 - 2 * (index % 2)) * turn],
            )
            for index in range(4)
        ]

    for part in range(2):
        gather_first(part)
    for part in range(4):
        alls[part][dom, sub] = owns[part][...]

    states = split(node_states[...])
    list_picks, list_back = picks_of(lists[...], node_rows)
    outgoing[...] = picked(list_back, states).reshape(4, ghost, width)
    ghost_copies = halo_copies(outgoing, ghosts, 0)
    for copy in ghost_copies:
        copy.start()
    target_picks, target_back = picks_of(endpoints[1:2, :], node_rows)
    source_picks, source_back = picks_of(endpoints[0:1, :], node_rows)
    ghost_picks, ghost_back = picks_of(endpoints[0:1, :], 4 * ghost, node_rows)
    live_nodes = jnp.where(
        lax.broadcasted_iota(jnp.int32, (node_rows, 1), 0) < counts[0], 1.0, 0.0
    ).astype(jnp.float32)
    live_edges = jnp.where(
        lax.broadcasted_iota(jnp.int32, (edge_rows, 1), 0) < blocks[0] * 128, 1.0, 0.0
    ).astype(jnp.float32)
    edge_act = split(jnp.maximum(edge_pre[...], 0.0))
    node_act = split(jnp.maximum(node_pre[...], 0.0))

    gather_from_sub(0)
    gather_first(2)
    gather_from_sub(1)
    gather_first(3)
    gather_from_x(0)
    gather_from_core(0)
    second_rows = width // (doms * subs)
    node_second = split(all_a[:, :, :second_rows, :].reshape(width, width))
    params = jnp.sum(
        all_a[:, :, second_rows:, :].reshape(doms * subs, -1, width), axis=0
    )
    edge_bias, edge_gain, edge_shift, node_bias, node_gain = (
        params[row : row + 1, :] for row in range(5)
    )
    node_normed, node_inverse = layer_norm(wide(node_act, node_second, (1, 0)) + node_bias)
    gather_from_x(1)
    gather_from_sub(2, [1])
    node_upstream = node_cotangent[...] * live_nodes
    node_grad_z = split(norm_back(node_upstream * node_gain, node_normed, node_inverse))
    gather_from_sub(2, range(2, subs))
    sum_b[...] = (wide(node_act, node_grad_z, (0, 0)) * node_scale).reshape(sum_b.shape)
    reduce_core(0)
    gather_from_core(1)
    edge_second = split(all_b[...].reshape(width, width))
    edge_normed, edge_inverse = layer_norm(wide(edge_act, edge_second, (1, 0)) + edge_bias)
    message = (edge_normed * edge_gain + edge_shift) * live_edges
    aggregate = split(picked(target_picks, split(message)))
    gather_from_x(2)
    gather_from_sub(3, [1])
    reduce_x(0)
    node_grad_pre = split(
        wide(node_grad_z, node_second, (1, 1)) * (node_pre[...] > 0).astype(jnp.float32)
    )
    gather_from_sub(3, range(2, subs))
    sum_c[: doms // 2] = (wide(states, node_grad_pre, (0, 0)) * node_scale).reshape(
        doms // 2, *sum_c.shape[1:]
    )
    gather_from_y(2)
    sum_c[doms // 2 :] = (wide(aggregate, node_grad_pre, (0, 0)) * node_scale).reshape(
        doms // 2, *sum_c.shape[1:]
    )
    reduce_core(1)
    reduce_core(2)
    gather_from_x(3)
    gather_from_core(2)
    reduce_x(1)
    reduce_x(2)

    node_first = split(all_c[...].reshape(2 * width, width))
    from_nodes = wide(
        node_grad_pre, tuple(half[width:] for half in node_first), (1, 1)
    )
    edge_upstream = (edge_cotangent[...] + picked(target_back, split(from_nodes))) * live_edges
    edge_grad_z = split(norm_back(edge_upstream * edge_gain, edge_normed, edge_inverse))
    sum_a[...] = (wide(edge_act, edge_grad_z, (0, 0)) * edge_scale).reshape(sum_a.shape)
    reduce_core(3)
    reduce_sub(0)
    gather_from_y(3)
    edge_grad_pre = split(
        wide(edge_grad_z, edge_second, (1, 1)) * (edge_pre[...] > 0).astype(jnp.float32)
    )
    for copy in ghost_copies:
        copy.wait_recv()
    sender = picked(source_back, states) + picked(
        ghost_back, split(ghosts[...].reshape(4 * ghost, width))
    )
    receiver = picked(target_back, states)
    reduce_x(3)
    reduce_sub(1)
    reduce_sub(2)
    first_grad = jnp.concatenate(
        [
            wide(split(feature), edge_grad_pre, (0, 0)) * edge_scale
            for feature in (edge_states[...], sender, receiver)
        ],
        axis=0,
    )
    sum_d[...] = first_grad.reshape(sum_d.shape)
    for unit in range(4, len(units)):
        reduce_core(unit)
    for unit in range(4, len(units)):
        reduce_x(unit)
    reduce_sub(3)
    state_grads = node_upstream + wide(
        node_grad_pre, tuple(half[:width] for half in node_first), (1, 1)
    )

    gather_from_core(3)
    edge_first = split(all_d[...].reshape(3 * width, width))

    def edge_part(index):
        rows = slice(index * width, (index + 1) * width)
        return wide(edge_grad_pre, tuple(half[rows] for half in edge_first), (1, 1))

    sender_grads = split(edge_part(1))
    ghost_grads[...] = picked(ghost_picks, sender_grads).reshape(4, ghost, width)
    return_copies = halo_copies(ghost_grads, returned, 1)
    for copy in return_copies:
        copy.start()
    reduce_sub(4)
    edge_grads[...] = (edge_cotangent[...] + edge_part(0)) * live_edges
    state_grads = state_grads + picked(source_picks, sender_grads)
    state_grads = state_grads + picked(target_picks, split(edge_part(2)))
    for unit in range(5, len(units)):
        reduce_sub(unit)
    for copy in return_copies:
        copy.wait_recv()
    node_grads[...] = state_grads + picked(
        list_picks, split(returned[...].reshape(4 * ghost, width))
    )
    for unit in range(len(units)):
        reduce_last(unit)

    for copy in pending + ghost_copies + return_copies:
        copy.wait_send()
    for unit in range(len(units)):
        for copy in core_copies(unit) + [x_copy(unit)] + sub_copies(unit):
            copy.wait_send()


def kernel_shards(
    node_states,
    node_pre,
    edge_states,
    edge_pre,
    node_cotangent,
    edge_cotangent,
    endpoints,
    send_lists,
    node_counts,
    edge_blocks,
    edge_first,
    edge_second,
    edge_bias,
    edge_gain,
    edge_shift,
    node_first,
    node_second,
    node_bias,
    node_gain,
):
    node_rows, width = node_states.shape
    edge_rows = edge_states.shape[0]
    ghost = send_lists.shape[2]
    doms, subs = lax.axis_size("dom"), lax.axis_size("sub")
    peers = doms * subs
    mine = lax.axis_index("dom") * subs + lax.axis_index("sub")
    place = jnp.arange(width) // (width // peers) == mine
    vectors = jnp.stack([edge_bias, edge_gain, edge_shift, node_bias, node_gain])
    spread = jnp.where(place[None, :], jnp.tile(vectors, (1, peers)), 0.0)
    own_a = jnp.concatenate([node_second, spread, jnp.zeros((3, width), jnp.float32)], axis=0)
    owns = (own_a, edge_second, node_first, edge_first)
    sums = (node_second, node_first, edge_second, edge_first)
    units = sum(shard.shape[0] for shard in sums) // UNIT
    vmem = pl.BlockSpec(memory_space=pltpu.VMEM)
    smem = pl.BlockSpec(memory_space=pltpu.SMEM)
    f32 = jnp.float32
    dma = pltpu.SemaphoreType.DMA
    halo = pltpu.VMEM((4, ghost, width), f32)
    return pl.pallas_call(
        functools.partial(
            layer_kernel,
            1.0 / math.sqrt(edge_rows * peers),
            1.0 / math.sqrt(node_rows * peers),
        ),
        out_shape=[
            jax.ShapeDtypeStruct(shape, f32)
            for shape in (
                edge_states.shape,
                node_states.shape,
                edge_first.shape,
                edge_second.shape,
                node_first.shape,
                node_second.shape,
            )
        ],
        in_specs=[smem, smem] + [vmem] * 12,
        out_specs=[vmem] * 6,
        scratch_shapes=[pltpu.VMEM((doms, subs) + own.shape, f32) for own in owns]
        + [pltpu.VMEM((doms, subs) + shard.shape, f32) for shard in sums]
        + [
            pltpu.VMEM((units, 2, subs, UNIT, width), f32),
            pltpu.VMEM((units, subs, UNIT, width), f32),
            pltpu.VMEM((units, subs - 1, UNIT, width), f32),
            halo,
            halo,
            halo,
            halo,
            dma((4, 8 * subs - 1)),
            dma((4, 8 * subs - 1)),
            dma((units, 2)),
            dma((units, 2)),
            dma((units,)),
            dma((units,)),
            dma((units, subs - 1)),
            dma((units, subs - 1)),
            dma((2, 4)),
            dma((2, 4)),
        ],
        compiler_params=pltpu.CompilerParams(
            collective_id=0, has_side_effects=True, vmem_limit_bytes=56 * 2**20
        ),
    )(
        node_counts,
        edge_blocks,
        endpoints,
        send_lists.reshape(1, 4 * ghost),
        node_states,
        node_pre,
        edge_states,
        edge_pre,
        node_cotangent,
        edge_cotangent,
        *owns,
    )


def shards(*blocks):
    weights = (blocks[10], blocks[11], blocks[15], blocks[16])
    fits = all(weight.shape[0] % UNIT == 0 for weight in weights)
    paired = lax.axis_size("groups") == 2 and lax.axis_size("dom") == 4
    if paired and lax.axis_size("sub") > 2 and fits:
        return tuple(kernel_shards(*blocks))
    return plain_shards(*blocks)


def solution(mesh):
    in_specs = (
        P(("groups", "dom", "sub"), None),
        P(("groups", "dom", "sub"), None),
        P(("groups", "dom", "sub"), None),
        P(("groups", "dom", "sub"), None),
        P(("groups", "dom", "sub"), None),
        P(("groups", "dom", "sub"), None),
        P(None, ("groups", "dom", "sub")),
        P(("groups", "dom", "sub"), None, None),
        P(("groups", "dom", "sub")),
        P(("groups", "dom", "sub")),
        P(("dom", "sub"), None),
        P(("dom", "sub"), None),
        P(("dom", "sub")),
        P(("dom", "sub")),
        P(("dom", "sub")),
        P(("dom", "sub"), None),
        P(("dom", "sub"), None),
        P(("dom", "sub")),
        P(("dom", "sub")),
    )
    out_specs = (
        P(("groups", "dom", "sub"), None),
        P(("groups", "dom", "sub"), None),
        P(("groups", "dom", "sub"), None),
        P(("groups", "dom", "sub"), None),
        P(("groups", "dom", "sub"), None),
        P(("groups", "dom", "sub"), None),
    )
    return jax.shard_map(shards, mesh=mesh, in_specs=in_specs, out_specs=out_specs, check_vma=False)
```
